128 devices in a mesh: shard: 4 (over y_lo, core), replica: 32 (over y_hi, z, x).
Axes of the slice: x: 4, y: 4 (y_hi: 2, y_lo: 2; y = y_hi * 2 + y_lo), z: 4, core: 2. Of those that a mesh axis runs over, the one named last changes fastest.
Arguments:
- tokens: bfloat16 [32, 1184, 1024], P('replica', 'shard'), may hold values from -6 to 6
- image_count: int32 [32], P('replica'), may hold values from 1 to 2, as said below
- cotangent: bfloat16 [32, 1184, 1024], P('replica', 'shard'), may hold values from -6 to 6
- ln1_gain: bfloat16 [1024], P('shard'), may hold values from 0.5 to 1.5
- ln1_bias: bfloat16 [1024], P('shard'), may hold values from -1.75 to 1.75
- w_qkv: bfloat16 [1024, 3072], P('shard'), may hold values from -0.1875 to 0.1875
- b_query: bfloat16 [1024], P('shard'), may hold values from -1.75 to 1.75
- b_value: bfloat16 [1024], P('shard'), may hold values from -1.75 to 1.75
- w_out: bfloat16 [1024, 1024], P('shard'), may hold values from -1 to 1
- b_out: bfloat16 [1024], P('shard'), may hold values from -1.75 to 1.75
- ln2_gain: bfloat16 [1024], P('shard'), may hold values from 0.5 to 1.5
- ln2_bias: bfloat16 [1024], P('shard'), may hold values from -1.75 to 1.75
- w_fc1: bfloat16 [1024, 4096], P('shard'), may hold values from -0.1875 to 0.1875
- b_fc1: bfloat16 [4096], P('shard'), may hold values from -1.75 to 1.75
- w_fc2: bfloat16 [4096, 1024], P('shard'), may hold values from -0.125 to 0.125
- b_fc2: bfloat16 [1024], P('shard'), may hold values from -1.75 to 1.75
Outputs:
- out_tokens: bfloat16 [32, 1184, 1024], P('replica', 'shard')
- grad_tokens: float32 [32, 1184, 1024], P('replica', 'shard')
- grad_ln1_gain: float32 [1024], P('shard')
- grad_ln1_bias: float32 [1024], P('shard')
- grad_w_qkv: float32 [1024, 3072], P('shard')
- grad_b_query: float32 [1024], P('shard')
- grad_b_value: float32 [1024], P('shard')
- grad_w_out: float32 [1024, 1024], P('shard')
- grad_b_out: float32 [1024], P('shard')
- grad_ln2_gain: float32 [1024], P('shard')
- grad_ln2_bias: float32 [1024], P('shard')
- grad_w_fc1: float32 [1024, 4096], P('shard')
- grad_b_fc1: float32 [4096], P('shard')
- grad_w_fc2: float32 [4096, 1024], P('shard')
- grad_b_fc2: float32 [1024], P('shard')
The draws below stay inside these ranges and needn't reach their ends.
Inputs may be any that keep to these rules, and one draw needn't show every extreme that they name: `image_count`: exactly 3 groups hold two images and the others one.
All inputs are finite; a program needn't handle non-finite values.
Results may differ from the reference program's by a relative error of at most 0.028.
Values may be sent and summed in bfloat16 or wider, within the bound.
No kernel may reach another device: no remote copies, remote signals or barrier semaphores. Data moves between devices by JAX's collectives and lax.ppermute only.
A program may use at most 192 MiB of HBM per device.

```python
import jax
import jax.numpy as jnp
from jax import lax

D = 1024
HEADS = 16
HEAD_DIM = 64
FF = 4096
IMG_LEN = 577
EXTRA = 3
GROUPS = 32
GROUP_ROWS = 1184


def draw_image_count(key, part):
    key = jax.random.fold_in(key, 7)
    order = jax.random.permutation(key, GROUPS)
    return (1 + (order < EXTRA)).astype(jnp.int32)


def steps_of(rng, dims, pieces, low, largest):
    def one(dim, parts):
        heights = jax.random.uniform(jax.random.fold_in(jax.random.fold_in(rng, 6), dim), (parts,), jnp.float32, low / len(pieces), largest / len(pieces))
        return jnp.repeat(jnp.exp(heights), dims[dim] // parts).reshape((-1,) + (1,) * (len(dims) - dim - 1))

    factor_of = one(*pieces[0])
    for cut in pieces[1:]:
        factor_of = factor_of * one(*cut)
    return factor_of


def normal_values(key, extent, spread, bound, shards=(), dtype=jnp.bfloat16):
    values = jax.random.normal(key, extent, jnp.float32) * spread
    if len(shards) > 0:
        values = steps_of(key, extent, shards, -0.22, 0.18) * values
    return jnp.clip(values, min=-bound, max=bound).astype(dtype)


def setup_inputs(seed: int = 0) -> dict:
    key_list = jax.random.split(jax.random.key(seed), 17)
    return {
        "tokens": normal_values(key_list[0], (GROUPS, GROUP_ROWS, D), 1.0, 6.0, ((0, 32), (1, 4))),
        "image_count": draw_image_count(jax.random.fold_in(key_list[16], 71), 0),
        "cotangent": normal_values(key_list[2], (GROUPS, GROUP_ROWS, D), 1.0, 6.0, ((0, 32), (1, 4))),
        "ln1_gain": jnp.clip(1.0 + 0.1 * jax.random.normal(key_list[3], (D,), jnp.float32), 0.5, 1.5).astype(jnp.bfloat16),
        "ln1_bias": normal_values(key_list[4], (D,), 0.3, 1.75, ((0, 4),)),
        "w_qkv": normal_values(key_list[5], (D, 3 * D), D ** -0.5, 0.1875, ((0, 4),)),
        "b_query": normal_values(key_list[6], (D,), 0.3, 1.75, ((0, 4),)),
        "b_value": normal_values(key_list[7], (D,), 0.3, 1.75, ((0, 4),)),
        "w_out": normal_values(key_list[8], (D, D), (max(D // 24, 1)) ** -0.5, 1.0, ((0, 4),)),
        "b_out": normal_values(key_list[9], (D,), 0.3, 1.75, ((0, 4),)),
        "ln2_gain": jnp.clip(1.0 + 0.1 * jax.random.normal(key_list[10], (D,), jnp.float32), 0.5, 1.5).astype(jnp.bfloat16),
        "ln2_bias": normal_values(key_list[11], (D,), 0.3, 1.75, ((0, 4),)),
        "w_fc1": normal_values(key_list[12], (D, FF), D ** -0.5, 0.1875, ((0, 4),)),
        "b_fc1": normal_values(key_list[13], (FF,), 0.3, 1.75, ((0, 4),)),
        "w_fc2": normal_values(key_list[14], (FF, D), (FF // 2) ** -0.5, 0.125, ((0, 4),)),
        "b_fc2": normal_values(key_list[15], (D,), 0.3, 1.75, ((0, 4),)),
    }


@jax.custom_vjp
def low(v):
    return lax.optimization_barrier(v.astype(jnp.bfloat16)).astype(jnp.float32)

@jax.custom_vjp
def low_back(v):
    return v

def low_keep(v):
    return (low(v), None)

def low_pass(kept, grad):
    return (grad,)

def back_keep(v):
    return (v, None)

def back_low(kept, grad):
    return (low(grad),)
low.defvjp(low_keep, low_pass)
low_back.defvjp(back_keep, back_low)

def norm(value, gain, shift):
    mean = lax.optimization_barrier(jnp.mean(value, axis=-1, keepdims=True))
    centred = value - mean
    variance = lax.optimization_barrier(jnp.mean(centred * centred, axis=-1, keepdims=True))
    return centred * lax.rsqrt(variance + 1e-06) * gain + shift

def matmul(left, right):
    return jnp.dot(left, right, precision=lax.Precision.HIGHEST)

def forward(value, params):
    ln1_gain, ln1_bias, w_qkv, b_query, b_value, w_out, b_out, ln2_gain, ln2_bias, w_fc1, b_fc1, w_fc2, b_fc2 = params
    slots = jnp.arange(GROUP_ROWS)
    image = slots // IMG_LEN
    same = image[:, None] == image[None, :]
    first = low(norm(value, ln1_gain, ln1_bias))
    packed = matmul(first, w_qkv)
    query = low(low_back(packed[:, :D] + b_query)).reshape(GROUP_ROWS, HEADS, HEAD_DIM)
    keys = low(low_back(packed[:, D:2 * D])).reshape(GROUP_ROWS, HEADS, HEAD_DIM)
    values = low(low_back(packed[:, 2 * D:] + b_value)).reshape(GROUP_ROWS, HEADS, HEAD_DIM)
    scores = low_back(0.125 * jnp.einsum('rhd,shd->hrs', query, keys, precision=lax.Precision.HIGHEST))
    scores = jnp.where(same[None], scores, -1e+30)
    weights = jax.nn.softmax(scores, axis=-1)
    attended = jnp.einsum('hrs,shd->rhd', low(weights), values, precision=lax.Precision.HIGHEST)
    attended = low(low_back(attended.reshape(GROUP_ROWS, D)))
    middle = value + low_back(matmul(attended, w_out) + b_out)
    second = low(norm(middle, ln2_gain, ln2_bias))
    hidden = low_back(matmul(second, w_fc1) + b_fc1)
    act = low(jax.nn.gelu(hidden, approximate=False))
    return middle + low_back(matmul(act, w_fc2) + b_fc2)

def reference(tokens, image_count, cotangent, ln1_gain, ln1_bias, w_qkv, b_query, b_value, w_out, b_out, ln2_gain, ln2_bias, w_fc1, b_fc1, w_fc2, b_fc2):
    params = tuple((p.astype(jnp.float32) for p in (ln1_gain, ln1_bias, w_qkv, b_query, b_value, w_out, b_out, ln2_gain, ln2_bias, w_fc1, b_fc1, w_fc2, b_fc2)))
    slots = jnp.arange(GROUP_ROWS)

    def one_group(totals, inputs):
        group_tokens, group_cot, count = inputs
        valid = (slots < count * IMG_LEN).astype(jnp.float32)
        result, pull = jax.vjp(forward, group_tokens.astype(jnp.float32), params)
        d_value, d_params = pull(group_cot.astype(jnp.float32) * valid[:, None])
        totals = jax.tree.map(lambda a, b: a + b, totals, d_params)
        return (totals, (result.astype(jnp.bfloat16), d_value))
    zeros = tuple((jnp.zeros(p.shape, jnp.float32) for p in params))
    grads, (outs, d_tokens) = lax.scan(one_group, zeros, (tokens, cotangent, image_count.astype(jnp.int32)))
    return (outs, d_tokens, grads[0], grads[1], grads[2], grads[3], grads[4], grads[5], grads[6], grads[7], grads[8], grads[9], grads[10], grads[11], grads[12])
```

```python
import jax
import jax.numpy as jnp
from jax import lax
from jax.experimental import pallas as pl
from jax.experimental.pallas import tpu as pltpu
from jax.sharding import PartitionSpec as P

HEAD_DIM = 64
IMG_LEN = 577
AXES = ("shard", "replica")
BF = jnp.bfloat16
F32 = jnp.float32
TAIL = 16


def place(index):
    shard, replica = divmod(index, 32)
    return (replica // 16) * 2 + shard // 2, (replica // 4) % 4, replica % 4, shard % 2


def index_of(y, z, x, core):
    y, z, x = y % 4, z % 4, x % 4
    return ((y % 2) * 2 + core) * 32 + (y // 2) * 16 + z * 4 + x


def moved(dy=0, dz=0, dx=0, dc=0):
    pairs = []
    for index in range(128):
        y, z, x, core = place(index)
        pairs.append((index, index_of(y + dy, z + dz, x + dx, (core + dc) % 2)))
    return pairs


CORE = moved(dc=1)
Y_UP = moved(dy=1)
Y_DOWN = moved(dy=-1)
Y_FAR = moved(dy=2)
X_BY = {d: moved(dx=d) for d in (1, 2, 3)}
Z_BY = {d: moved(dz=d) for d in (1, 2, 3)}
TO_FIRST = [(32 + r, 64 + r) for r in range(32)]
TO_SECOND = [(32 + r, 96 + r) for r in range(32)]
TAIL_BACK = [(96 + r, 32 + r) for r in range(32)]


def send(value, pairs):
    return lax.ppermute(value, AXES, pairs)


def dot(left, right, dims=((1,), (0,))):
    return lax.dot_general(left, right, (dims, ((), ())), preferred_element_type=F32)


def normed(value):
    mean = jnp.mean(value, axis=-1, keepdims=True)
    centred = value - mean
    variance = jnp.mean(centred * centred, axis=-1, keepdims=True)
    scale = lax.rsqrt(variance + 1e-06)
    return centred * scale, scale


def norm_back(d_value, unit, scale, gain):
    t = d_value * gain
    mean_t = jnp.mean(t, axis=-1, keepdims=True)
    mean_tn = jnp.mean(t * unit, axis=-1, keepdims=True)
    return scale * (t - mean_t - unit * mean_tn)


def attend_kernel(id_col, id_row, q_ref, k_ref, v_ref, out_ref, w_ref):
    q, k, v = q_ref[...], k_ref[...], v_ref[...]
    first_head = lax.broadcasted_iota(jnp.int32, q.shape, 1) < HEAD_DIM
    same = id_col[...] == id_row[...]
    zero = jnp.zeros_like(q)
    results = []
    for head in range(2):
        mine = first_head if head == 0 else jnp.logical_not(first_head)
        scores = 0.125 * dot(jnp.where(mine, q, zero), k, ((1,), (1,)))
        scores = jnp.where(same, scores, -1e30)
        peak = jnp.max(scores, axis=-1, keepdims=True)
        expo = jnp.exp(scores - peak)
        total = jnp.sum(expo, axis=-1, keepdims=True)
        weights = (expo * (1.0 / total)).astype(BF)
        w_ref[head] = weights
        results.append(dot(weights, v))
    out_ref[...] = jnp.where(first_head, results[0], results[1]).astype(BF)


def attend(ids, qkv):
    rows = qkv.shape[0]
    pairs = qkv.shape[1] // 3 // 128
    block = lambda off: pl.BlockSpec((rows, 128), lambda h: (0, h + off))
    return pl.pallas_call(
        attend_kernel,
        grid=(pairs,),
        in_specs=[
            pl.BlockSpec((rows, 1), lambda h: (0, 0)),
            pl.BlockSpec((1, rows), lambda h: (0, 0)),
            block(0),
            block(pairs),
            block(2 * pairs),
        ],
        out_specs=[block(0), pl.BlockSpec((2, rows, rows), lambda h: (h, 0, 0))],
        out_shape=[
            jax.ShapeDtypeStruct((rows, pairs * 128), BF),
            jax.ShapeDtypeStruct((2 * pairs, rows, rows), BF),
        ],
        compiler_params=pltpu.CompilerParams(vmem_limit_bytes=48 * 2**20),
        cost_estimate=pl.CostEstimate(
            flops=16 * pairs * rows * rows * 128, bytes_accessed=8 * 2**20, transcendentals=0
        ),
    )(ids[:, None], ids[None, :], qkv, qkv, qkv)


def attend_back_kernel(q_ref, k_ref, v_ref, d_ref, w_ref, dq_ref, dk_ref, dv_ref):
    q, k, v, d_out = q_ref[...], k_ref[...], v_ref[...], d_ref[...]
    first_head = lax.broadcasted_iota(jnp.int32, q.shape, 1) < HEAD_DIM
    zero = jnp.zeros_like(q)
    parts = []
    for head in range(2):
        mine = first_head if head == 0 else jnp.logical_not(first_head)
        low = w_ref[head]
        weights = low.astype(F32)
        d_weights = dot(jnp.where(mine, d_out, zero), v, ((1,), (1,)))
        both = weights * d_weights
        d_scores = (both - weights * jnp.sum(both, axis=-1, keepdims=True)).astype(BF)
        parts.append(
            (
                dot(d_scores, k),
                dot(d_scores, q, ((0,), (0,))),
                dot(low, d_out, ((0,), (0,))),
            )
        )
    dq_ref[...] = (0.125 * jnp.where(first_head, parts[0][0], parts[1][0])).astype(BF)
    dk_ref[...] = (0.125 * jnp.where(first_head, parts[0][1], parts[1][1])).astype(BF)
    dv_ref[...] = jnp.where(first_head, parts[0][2], parts[1][2]).astype(BF)


def attend_back(qkv, d_att, weights):
    rows = qkv.shape[0]
    pairs = qkv.shape[1] // 3 // 128
    block = lambda off: pl.BlockSpec((rows, 128), lambda h: (0, h + off))
    return pl.pallas_call(
        attend_back_kernel,
        grid=(pairs,),
        in_specs=[
            block(0),
            block(pairs),
            block(2 * pairs),
            block(0),
            pl.BlockSpec((2, rows, rows), lambda h: (h, 0, 0)),
        ],
        out_specs=[block(0)] * 3,
        out_shape=[jax.ShapeDtypeStruct((rows, pairs * 128), BF)] * 3,
        compiler_params=pltpu.CompilerParams(vmem_limit_bytes=48 * 2**20),
        cost_estimate=pl.CostEstimate(
            flops=32 * pairs * rows * rows * 128, bytes_accessed=10 * 2**20, transcendentals=0
        ),
    )(qkv, qkv, qkv, d_att, weights)


def body(
    tokens,
    image_count,
    cotangent,
    ln1_gain,
    ln1_bias,
    w_qkv,
    b_query,
    b_value,
    w_out,
    b_out,
    ln2_gain,
    ln2_bias,
    w_fc1,
    b_fc1,
    w_fc2,
    b_fc2,
):
    shard = lax.axis_index("shard")
    replica = lax.axis_index("replica")
    y_lo, core = shard // 2, shard % 2
    x_at, z_at = replica % 4, (replica // 4) % 4
    width = tokens.shape[2]
    rows_dev = tokens.shape[1]
    rows = 2 * rows_dev + TAIL
    mine = rows_dev + TAIL

    def ordered(flag, own, other, axis=0):
        return jnp.where(
            flag == 0,
            jnp.concatenate([own, other], axis),
            jnp.concatenate([other, own], axis),
        )

    def by_core(w, blocks, part):
        view = w.reshape(w.shape[0], blocks, 2, -1)
        return lax.dynamic_index_in_dim(view, part, 2, keepdims=False).reshape(w.shape[0], -1)

    def chip_half(w, blocks):
        kept = by_core(w, blocks, core)
        got = send(by_core(w, blocks, 1 - core), CORE)
        return jnp.where(core == 0, kept, got), jnp.where(core == 0, got, kept)

    def across(low, high):
        return send(low, Y_UP), send(high, Y_DOWN)

    small = jnp.stack(
        [ln1_gain, ln1_bias, b_query, b_value, b_out, ln2_gain, ln2_bias, b_fc2]
        + [b_fc1[256 * k : 256 * k + 256] for k in range(4)]
    )
    small = lax.all_gather(small, "shard", axis=0).astype(F32)
    vector = lambda k: small[:, k].reshape(-1)
    core_part = lambda v: lax.dynamic_index_in_dim(
        v.reshape(2, 2, -1), core, 1, keepdims=False
    ).reshape(-1)
    gain_1, shift_1, bias_out = vector(0), vector(1), vector(4)
    gain_2, shift_2, bias_down = vector(5), vector(6), vector(7)
    bias_query, bias_value = core_part(vector(2)), core_part(vector(3))
    bias_up = core_part(small[:, 8:12].reshape(-1))

    own = jnp.stack([tokens[0], cotangent[0]])
    other = send(own, CORE)
    tail = own[:, rows_dev - TAIL :]
    tail_low, tail_high = send(tail, TO_FIRST), send(tail, TO_SECOND)
    tail = jnp.where(core == 0, tail_low, tail_high)

    q_low, q_high = chip_half(w_qkv, 6)
    q_got = across(q_low, q_high)
    o_got = across(w_out[:128], w_out[128:])
    u_low, u_high = chip_half(w_fc1, 2)
    u_low, u_high, _ = lax.optimization_barrier((u_low, u_high, q_got))
    u_got = across(u_low, u_high)
    d_low, d_high, _ = lax.optimization_barrier((w_fc2[:512], w_fc2[512:], o_got))
    d_got = across(d_low, d_high)

    cat = lambda pair: jnp.concatenate(pair, 0)
    proj_qkv = ordered(y_lo, cat((q_low, q_high)), cat(q_got))
    proj_out = ordered(y_lo, w_out, cat(o_got))
    proj_up = ordered(y_lo, cat((u_low, u_high)), cat(u_got))
    proj_down = ordered(y_lo, cat((d_low, d_high)), cat(d_got))

    everything = jnp.concatenate([ordered(core, own, other, 1), tail], axis=1)
    at = jnp.arange(rows)
    chip_rows = 2 * rows_dev
    second_end = 2 * IMG_LEN - chip_rows
    ids_first = jnp.where(at < IMG_LEN, 0, 1)
    ids_second = jnp.where(
        (at < second_end) | (at > chip_rows), 0, jnp.where(at == chip_rows, 2, 1)
    )
    ids = jnp.where(y_lo == 0, ids_first, ids_second)
    valid = ((ids == 0) & (image_count[0] > y_lo)).astype(F32)

    value = everything[0].astype(F32)
    unit_1, scale_1 = normed(value)
    first = (unit_1 * gain_1 + shift_1).astype(BF)
    packed = dot(first, proj_qkv)
    qkv = (packed + jnp.concatenate([bias_query, jnp.zeros_like(bias_query), bias_value])).astype(
        BF
    )
    attended, weights = attend(ids, qkv)
    z_part = dot(attended, proj_out)
    middle = value + z_part + send(z_part.astype(BF), CORE).astype(F32) + bias_out
    unit_2, scale_2 = normed(middle)
    second = (unit_2 * gain_2 + shift_2).astype(BF)
    hidden = dot(second, proj_up) + bias_up
    cdf = 0.5 * (1.0 + lax.erf(hidden * (0.5**0.5)))
    act = (hidden * cdf).astype(BF)
    slope = (cdf + hidden * (0.3989422804014327 * jnp.exp(-0.5 * hidden * hidden))).astype(BF)

    pick = lambda v, who: lax.dynamic_slice_in_dim(v, who * rows_dev, mine, 0)
    y_part = dot(act, proj_down)
    y_got = send(pick(y_part, 1 - core).astype(BF), CORE)
    out = (pick(middle, core) + pick(y_part, core) + y_got.astype(F32) + bias_down).astype(BF)

    d_out = everything[1].astype(F32) * valid[:, None]
    d_low_out = d_out.astype(BF)
    grad_down = dot(act, d_low_out, ((0,), (0,))).astype(BF)
    d_act = dot(d_low_out, proj_down, ((1,), (1,)))
    d_hidden = (d_act * slope.astype(F32)).astype(BF)
    grad_up = dot(second, d_hidden, ((0,), (0,))).astype(BF)
    d_second = dot(d_hidden, proj_up, ((1,), (1,)))
    d_second = d_second + send(d_second.astype(BF), CORE).astype(F32)
    d_middle = d_out + norm_back(d_second, unit_2, scale_2, gain_2)
    d_branch = d_middle.astype(BF)
    grad_out = dot(attended, d_branch, ((0,), (0,))).astype(BF)
    d_attended = dot(d_branch, proj_out, ((1,), (1,))).astype(BF)
    d_qkv = jnp.concatenate(attend_back(qkv, d_attended, weights), axis=1)
    grad_qkv = dot(first, d_qkv, ((0,), (0,))).astype(BF)
    d_first = dot(d_qkv, proj_qkv, ((1,), (1,)))
    d_first_got = send(pick(d_first, 1 - core).astype(BF), CORE)
    d_first = pick(d_first, core) + d_first_got.astype(F32)
    unit_1, scale_1 = pick(unit_1, core), pick(scale_1, core)
    grad_tokens = pick(d_middle, core) + norm_back(d_first, unit_1, scale_1, gain_1)

    out_tail = send(out[rows_dev:], TAIL_BACK)
    grad_tail = send(grad_tokens[rows_dev:], TAIL_BACK)
    local = jnp.arange(rows_dev)[:, None] + rows_dev
    swapped = (shard == 1) & (local >= IMG_LEN)

    def with_tail(v, last):
        wide = jnp.concatenate([v[: rows_dev - TAIL], last], axis=0)
        return jnp.where(swapped, wide, v[:rows_dev])[None]

    out_tokens = with_tail(out, out_tail)
    grad_tokens = with_tail(grad_tokens, grad_tail)

    def ring_sum(v, at, by):
        step = v.shape[1] // 4
        chunk = lambda d: lax.dynamic_slice_in_dim(v, ((at + d) % 4) * step, step, 1)
        total = chunk(0).astype(F32)
        for d in (1, 3, 2):
            total = total + send(chunk(d), by[d]).astype(F32)
        return total.astype(BF)

    def ring_gather(v, at, by):
        pieces = [v] + [send(v, by[d]) for d in (1, 2, 3)]
        return jnp.concatenate(
            [lax.select_n((at - p) % 4, *pieces) for p in range(4)], axis=1
        )

    def chip_sum(grad, x_first, exchange):
        half = grad.shape[2] // 2
        kept = lax.dynamic_index_in_dim(grad, y_lo, 0, keepdims=False)
        given = lax.dynamic_index_in_dim(grad, 1 - y_lo, 0, keepdims=False)
        low = send(given[:, :half], Y_UP)
        high = send(given[:, half:], Y_DOWN)
        v = (kept.astype(F32) + jnp.concatenate([low, high], 1).astype(F32)).astype(BF)
        ways = [(x_at, X_BY), (z_at, Z_BY)]
        if not x_first:
            ways = ways[::-1]
        for way in ways:
            v = ring_sum(v, *way)
        v = (v.astype(F32) + send(v, Y_FAR).astype(F32)).astype(BF)
        if exchange:
            kept = lax.dynamic_index_in_dim(v, core, 0)
            got = send(lax.dynamic_index_in_dim(v, 1 - core, 0), CORE)
            v = ordered(core, kept, got, 0)
        for way in ways[::-1]:
            v = ring_gather(v, *way)
        return v.astype(F32)

    total_down = chip_sum(grad_down.reshape(2, 1, 1024, 1024), True, False)[0]
    total_up = chip_sum(grad_up.reshape(2, 2, 256, 2048), False, True)
    total_up = total_up.reshape(2, 256, 2, 1024).transpose(1, 2, 0, 3).reshape(256, 4096)
    total_out = chip_sum(grad_out.reshape(2, 1, 256, 1024), False, False)[0]
    total_qkv = chip_sum(grad_qkv.reshape(2, 2, 256, 1536), True, True)
    total_qkv = total_qkv.reshape(2, 256, 6, 256).transpose(1, 2, 0, 3).reshape(256, 3072)

    once = (core == 0).astype(F32)
    hot = (jnp.arange(2) == core).astype(F32)[None, :, None]
    spread = lambda v: (v.reshape(2, 1, -1) * hot).reshape(-1)
    kept_rows = (jnp.arange(mine) < rows_dev + TAIL * core).astype(F32)[:, None]
    d_first_kept = d_first * kept_rows
    over = lambda v: jnp.sum(v, axis=0)
    d_qkv_f = over(d_qkv.astype(F32))
    sums = jnp.concatenate(
        [
            over(d_first_kept * unit_1),
            over(d_first_kept),
            spread(d_qkv_f[:512]),
            spread(d_qkv_f[1024:]),
            once * over(d_branch.astype(F32)),
            once * over(d_second * unit_2),
            once * over(d_second),
            once * over(d_out),
            spread(over(d_hidden.astype(F32))),
        ]
    )
    sums = lax.psum(sums.reshape(12, 1024), AXES)
    vec = lambda k: lax.dynamic_slice_in_dim(sums[k], shard * 256, 256, 0)
    grad_up_bias = lax.dynamic_slice_in_dim(sums[8:].reshape(-1), shard * 1024, 1024, 0)
    return (
        out_tokens,
        grad_tokens,
        vec(0),
        vec(1),
        total_qkv,
        vec(2),
        vec(3),
        total_out,
        vec(4),
        vec(5),
        vec(6),
        total_up,
        grad_up_bias,
        total_down,
        vec(7),
    )


def solution(mesh):
    tokens, row, both = P("replica", "shard", None), P("shard"), P("shard", None)
    in_specs = (
        tokens, P("replica"), tokens, row, row, both, row, row, both, row, row, row, both, row,
        both, row,
    )
    out_specs = (
        tokens, tokens, row, row, both, row, row, both, row, row, row, both, row, both, row,
    )
    return jax.shard_map(body, mesh=mesh, in_specs=in_specs, out_specs=out_specs, check_vma=False)
```

```python
import jax
import jax.numpy as jnp
from jax import lax
from jax.experimental import pallas as pl
from jax.experimental.pallas import tpu as pltpu
from jax.sharding import PartitionSpec as P

HEAD_DIM = 64
IMG_LEN = 577
AXES = ("shard", "replica")
BF = jnp.bfloat16
F32 = jnp.float32
TAIL = 16


def place(index):
    shard, replica = divmod(index, 32)
    return (replica // 16) * 2 + shard // 2, (replica // 4) % 4, replica % 4, shard % 2


def index_of(y, z, x, core):
    y, z, x = y % 4, z % 4, x % 4
    return ((y % 2) * 2 + core) * 32 + (y // 2) * 16 + z * 4 + x


def moved(dy=0, dz=0, dx=0, dc=0):
    pairs = []
    for index in range(128):
        y, z, x, core = place(index)
        pairs.append((index, index_of(y + dy, z + dz, x + dx, (core + dc) % 2)))
    return pairs


CORE = moved(dc=1)
Y_UP = moved(dy=1)
Y_DOWN = moved(dy=-1)
Y_FAR = moved(dy=2)
FAR_CORE = moved(dy=2, dc=1)
X_BY = {d: moved(dx=d) for d in (1, 2, 3)}
Z_BY = {d: moved(dz=d) for d in (1, 2, 3)}
X_WITH = {d: [(i, index_of(y, z, x ^ d, c)) for i, (y, z, x, c) in enumerate(map(place, range(128)))] for d in (1, 3)}
Z_WITH = {d: [(i, index_of(y, z ^ d, x, c)) for i, (y, z, x, c) in enumerate(map(place, range(128)))] for d in (1, 3)}
PLANE = [[16 * h + k for k in range(16)] for h in range(2)]
TO_FIRST = [(32 + r, 64 + r) for r in range(32)]
TO_SECOND = [(32 + r, 96 + r) for r in range(32)]
TAIL_BACK = [(96 + r, 32 + r) for r in range(32)]


def after(value, *earlier):
    return lax.optimization_barrier((value, earlier))[0]


def send(value, pairs):
    return lax.ppermute(value, AXES, pairs)


def dot(left, right, dims=((1,), (0,))):
    return lax.dot_general(left, right, (dims, ((), ())), preferred_element_type=F32)


def normed(value):
    mean = jnp.mean(value, axis=-1, keepdims=True)
    centred = value - mean
    variance = jnp.mean(centred * centred, axis=-1, keepdims=True)
    scale = lax.rsqrt(variance + 1e-06)
    return centred * scale, scale


def norm_back(d_value, unit, scale, gain):
    t = d_value * gain
    mean_t = jnp.mean(t, axis=-1, keepdims=True)
    mean_tn = jnp.mean(t * unit, axis=-1, keepdims=True)
    return scale * (t - mean_t - unit * mean_tn)


def attend_kernel(id_col, id_row, q_ref, k_ref, v_ref, out_ref, w_ref):
    q, k, v = q_ref[...], k_ref[...], v_ref[...]
    first_head = lax.broadcasted_iota(jnp.int32, q.shape, 1) < HEAD_DIM
    same = id_col[...] == id_row[...]
    zero = jnp.zeros_like(q)
    results = []
    for head in range(2):
        mine = first_head if head == 0 else jnp.logical_not(first_head)
        scores = 0.125 * dot(jnp.where(mine, q, zero), k, ((1,), (1,)))
        scores = jnp.where(same, scores, -1e30)
        peak = jnp.max(scores, axis=-1, keepdims=True)
        expo = jnp.exp(scores - peak)
        total = jnp.sum(expo, axis=-1, keepdims=True)
        weights = (expo * (1.0 / total)).astype(BF)
        w_ref[head] = weights
        results.append(dot(weights, v))
    out_ref[...] = jnp.where(first_head, results[0], results[1]).astype(BF)


def attend(ids, qkv):
    rows = qkv.shape[0]
    pairs = qkv.shape[1] // 3 // 128
    block = lambda off: pl.BlockSpec((rows, 128), lambda h: (0, h + off))
    return pl.pallas_call(
        attend_kernel,
        grid=(pairs,),
        in_specs=[
            pl.BlockSpec((rows, 1), lambda h: (0, 0)),
            pl.BlockSpec((1, rows), lambda h: (0, 0)),
            block(0),
            block(pairs),
            block(2 * pairs),
        ],
        out_specs=[block(0), pl.BlockSpec((2, rows, rows), lambda h: (h, 0, 0))],
        out_shape=[
            jax.ShapeDtypeStruct((rows, pairs * 128), BF),
            jax.ShapeDtypeStruct((2 * pairs, rows, rows), BF),
        ],
        compiler_params=pltpu.CompilerParams(vmem_limit_bytes=48 * 2**20),
        cost_estimate=hinted(rows * rows),
    )(ids[:, None], ids[None, :], qkv, qkv, qkv)


def attend_back_kernel(q_ref, k_ref, v_ref, d_ref, w_ref, dq_ref, dk_ref, dv_ref):
    q, k, v, d_out = q_ref[...], k_ref[...], v_ref[...], d_ref[...]
    first_head = lax.broadcasted_iota(jnp.int32, q.shape, 1) < HEAD_DIM
    zero = jnp.zeros_like(q)
    parts = []
    for head in range(2):
        mine = first_head if head == 0 else jnp.logical_not(first_head)
        low = w_ref[head]
        weights = low.astype(F32)
        d_weights = dot(jnp.where(mine, d_out, zero), v, ((1,), (1,)))
        both = weights * d_weights
        d_scores = (both - weights * jnp.sum(both, axis=-1, keepdims=True)).astype(BF)
        parts.append(
            (
                dot(d_scores, k),
                dot(d_scores, q, ((0,), (0,))),
                dot(low, d_out, ((0,), (0,))),
            )
        )
    dq_ref[...] = (0.125 * jnp.where(first_head, parts[0][0], parts[1][0])).astype(BF)
    dk_ref[...] = (0.125 * jnp.where(first_head, parts[0][1], parts[1][1])).astype(BF)
    dv_ref[...] = jnp.where(first_head, parts[0][2], parts[1][2]).astype(BF)


def attend_back(qkv, d_att, weights):
    rows = qkv.shape[0]
    pairs = qkv.shape[1] // 3 // 128
    block = lambda off: pl.BlockSpec((rows, 128), lambda h: (0, h + off))
    return pl.pallas_call(
        attend_back_kernel,
        grid=(pairs,),
        in_specs=[
            block(0),
            block(pairs),
            block(2 * pairs),
            block(0),
            pl.BlockSpec((2, rows, rows), lambda h: (h, 0, 0)),
        ],
        out_specs=[block(0)] * 3,
        out_shape=[jax.ShapeDtypeStruct((rows, pairs * 128), BF)] * 3,
        compiler_params=pltpu.CompilerParams(vmem_limit_bytes=48 * 2**20),
        cost_estimate=hinted(rows * rows),
    )(qkv, qkv, qkv, d_att, weights)


def product_kernel(dims, a_ref, b_ref, *outs):
    total = dot(a_ref[...], b_ref[...], dims)
    for out in outs:
        out[...] = total.astype(out.dtype)


def hinted(flops):
    return pl.CostEstimate(flops=flops, bytes_accessed=0, transcendentals=0)


PARAMS = pltpu.CompilerParams(vmem_limit_bytes=48 * 2**20)


def times(a, b, tile, dtypes):
    rows, depth = a.shape
    cols = b.shape[1]
    return pl.pallas_call(
        lambda *refs: product_kernel(((1,), (0,)), *refs),
        grid=(cols // tile,),
        in_specs=[
            pl.BlockSpec((rows, depth), lambda i: (0, 0)),
            pl.BlockSpec((depth, tile), lambda i: (0, i)),
        ],
        out_specs=[pl.BlockSpec((rows, tile), lambda i: (0, i))] * len(dtypes),
        out_shape=[jax.ShapeDtypeStruct((rows, cols), t) for t in dtypes],
        compiler_params=PARAMS,
        cost_estimate=hinted(rows * depth),
    )(a, b)


def times_rows(a, b, tile, dtypes):
    rows, depth = a.shape
    cols = b.shape[0]
    return pl.pallas_call(
        lambda *refs: product_kernel(((1,), (1,)), *refs),
        grid=(cols // tile,),
        in_specs=[
            pl.BlockSpec((rows, depth), lambda i: (0, 0)),
            pl.BlockSpec((tile, depth), lambda i: (i, 0)),
        ],
        out_specs=[pl.BlockSpec((rows, tile), lambda i: (0, i))] * len(dtypes),
        out_shape=[jax.ShapeDtypeStruct((rows, cols), t) for t in dtypes],
        compiler_params=PARAMS,
        cost_estimate=hinted(rows * depth),
    )(a, b)


def grad_of(half, a, b, tile, side):
    rows, depth = a.shape
    cols = b.shape[1]
    tiles = depth // tile
    quarter = tiles // 4

    def kernel(half_ref, a_ref, b_ref, low, high, kept):
        i = pl.program_id(0)
        total = dot(a_ref[...], b_ref[...], ((0,), (0,))).astype(BF)

        if side:

            @pl.when(i < 2)
            def _():
                low[...] = total[: tile // 2]
                high[...] = total[tile // 2 :]

        else:

            @pl.when(i < quarter)
            def _():
                low[...] = total

            @pl.when((i >= quarter) & (i < 2 * quarter))
            def _():
                high[...] = total

        @pl.when(i >= tiles // 2)
        def _():
            kept[...] = total

    if side:
        specs = [
            pl.BlockSpec((tile // 2, cols), lambda i, h: (0, jnp.minimum(i, 1))),
            pl.BlockSpec((tile // 2, cols), lambda i, h: (0, jnp.minimum(i, 1))),
            pl.BlockSpec((tile, cols), lambda i, h: (0, jnp.maximum(i - 2, 0))),
        ]
        shapes = [(tile // 2, 2 * cols), (tile // 2, 2 * cols), (tile, 2 * cols)]
    else:
        specs = [
            pl.BlockSpec((tile, cols), lambda i, h: (jnp.minimum(i, quarter - 1), 0)),
            pl.BlockSpec((tile, cols), lambda i, h: (jnp.clip(i - quarter, 0, quarter - 1), 0)),
            pl.BlockSpec((tile, cols), lambda i, h: (jnp.maximum(i - 2 * quarter, 0), 0)),
        ]
        shapes = [(depth // 4, cols), (depth // 4, cols), (depth // 2, cols)]
    return pl.pallas_call(
        kernel,
        grid_spec=pltpu.PrefetchScalarGridSpec(
            num_scalar_prefetch=1,
            grid=(tiles,),
            in_specs=[
                pl.BlockSpec((rows, tile), lambda i, h: (0, (i + h[0] * (tiles // 2)) % tiles)),
                pl.BlockSpec((rows, cols), lambda i, h: (0, 0)),
            ],
            out_specs=specs,
        ),
        out_shape=[jax.ShapeDtypeStruct(t, BF) for t in shapes],
        compiler_params=PARAMS,
        cost_estimate=hinted(rows * depth),
    )(half, a, b)


def hidden_back(a, b, slope, tile):
    rows, depth = a.shape
    cols = b.shape[0]

    def kernel(a_ref, b_ref, slope_ref, out, sums):
        total = dot(a_ref[...], b_ref[...], ((1,), (1,))) * slope_ref[...].astype(F32)
        low = total.astype(BF)
        out[...] = low
        sums[...] = jnp.sum(low.astype(F32), axis=0, keepdims=True)

    return pl.pallas_call(
        kernel,
        grid=(cols // tile,),
        in_specs=[
            pl.BlockSpec((rows, depth), lambda i: (0, 0)),
            pl.BlockSpec((tile, depth), lambda i: (i, 0)),
            pl.BlockSpec((rows, tile), lambda i: (0, i)),
        ],
        out_specs=[
            pl.BlockSpec((rows, tile), lambda i: (0, i)),
            pl.BlockSpec((1, tile), lambda i: (0, i)),
        ],
        out_shape=[
            jax.ShapeDtypeStruct((rows, cols), BF),
            jax.ShapeDtypeStruct((1, cols), F32),
        ],
        compiler_params=PARAMS,
        cost_estimate=hinted(rows * depth),
    )(a, b, slope)


def body(
    tokens,
    image_count,
    cotangent,
    ln1_gain,
    ln1_bias,
    w_qkv,
    b_query,
    b_value,
    w_out,
    b_out,
    ln2_gain,
    ln2_bias,
    w_fc1,
    b_fc1,
    w_fc2,
    b_fc2,
):
    shard = lax.axis_index("shard")
    replica = lax.axis_index("replica")
    y_lo, core = shard // 2, shard % 2
    x_at, z_at = replica % 4, (replica // 4) % 4
    width = tokens.shape[2]
    rows_dev = tokens.shape[1]
    rows = 2 * rows_dev + TAIL
    mine = rows_dev + TAIL

    def ordered(flag, own, other, axis=0):
        return jnp.where(
            flag == 0,
            jnp.concatenate([own, other], axis),
            jnp.concatenate([other, own], axis),
        )

    cat = lambda parts, axis=0: jnp.concatenate(parts, axis)

    def blocks_of(w, size, parity):
        return cat([w[:, k : k + size] for k in range(parity * size, w.shape[1], 2 * size)], 1)

    def by_core(w, size, part):
        return jnp.where(part == 0, blocks_of(w, size, 0), blocks_of(w, size, 1))

    def across(w):
        half = w.shape[0] // 2
        return send(w[:half], Y_UP), send(w[half:], Y_DOWN)

    def columns(w, got, size):
        there = cat(got)
        pair = send(cat([by_core(w, size, 1 - core), by_core(there, size, 1 - core)]), CORE)
        rows_one = w.shape[0]
        here = ordered(core, by_core(w, size, core), pair[:rows_one])
        there = ordered(core, by_core(there, size, core), pair[rows_one:])
        return ordered(y_lo, here, there)

    own = (tokens[0], cotangent[0])
    q_got = across(w_qkv)
    other_tokens = send(own[0], CORE)
    own_tail = jnp.stack([v[rows_dev - TAIL :] for v in own])
    tail_low, tail_high = send(own_tail, TO_FIRST), send(own_tail, TO_SECOND)
    u_got = across(after(w_fc1, q_got))
    w_qkv, tail_low, own_tokens = after((w_qkv, tail_low, own[0]), q_got)
    own = (own_tokens, own[1])

    small = jnp.stack(
        [ln1_gain, ln1_bias, b_query, b_value, b_out, ln2_gain, ln2_bias, b_fc2]
        + [b_fc1[256 * k : 256 * k + 256] for k in range(4)]
    )
    small = lax.all_gather(small, "shard", axis=0).astype(F32)
    vector = lambda k: small[:, k].reshape(-1)
    core_part = lambda v: by_core(v[None], v.shape[0] // 4, core)[0]
    gain_1, shift_1, bias_out = vector(0), vector(1), vector(4)
    gain_2, shift_2, bias_down = vector(5), vector(6), vector(7)
    bias_query, bias_value = core_part(vector(2)), core_part(vector(3))
    bias_up = core_part(small[:, 8:12].reshape(-1))

    tail = jnp.where(core == 0, tail_low, tail_high)
    proj_qkv = columns(w_qkv, q_got, 256)
    whole = lambda k, other: cat([ordered(core, own[k], other), tail[k]])
    at = jnp.arange(rows)
    chip_rows = 2 * rows_dev
    second_end = 2 * IMG_LEN - chip_rows
    ids_first = jnp.where(at < IMG_LEN, 0, 1)
    ids_second = jnp.where(
        (at < second_end) | (at > chip_rows), 0, jnp.where(at == chip_rows, 2, 1)
    )
    ids = jnp.where(y_lo == 0, ids_first, ids_second)
    valid = ((ids == 0) & (image_count[0] > y_lo)).astype(F32)

    value = whole(0, other_tokens).astype(F32)
    unit_1, scale_1 = normed(value)
    first = (unit_1 * gain_1 + shift_1).astype(BF)
    packed = dot(first, proj_qkv)
    qkv = (packed + jnp.concatenate([bias_query, jnp.zeros_like(bias_query), bias_value])).astype(
        BF
    )
    o_got = across(after(w_out, qkv))
    cot_other = send(after(own[1], qkv), CORE)
    attended, weights = attend(ids, qkv)
    proj_out = ordered(y_lo, w_out, cat(o_got))
    u_got = after(u_got, attended)
    d_got = across(after(w_fc2, u_got))
    proj_up = columns(w_fc1, u_got, 1024)
    z_part = dot(attended, proj_out)
    middle = value + z_part + send(z_part.astype(BF), CORE).astype(F32) + bias_out
    unit_2, scale_2 = normed(middle)
    second = (unit_2 * gain_2 + shift_2).astype(BF)
    hidden = dot(second, proj_up) + bias_up
    cdf = 0.5 * (1.0 + lax.erf(hidden * (0.5**0.5)))
    act = (hidden * cdf).astype(BF)
    slope = (cdf + hidden * (0.3989422804014327 * jnp.exp(-0.5 * hidden * hidden))).astype(BF)

    pick = lambda v, who: lax.dynamic_slice_in_dim(v, who * rows_dev, mine, 0)
    d_out = whole(1, cot_other).astype(F32) * valid[:, None]
    d_low_out = d_out.astype(BF)
    half = (1 - y_lo).reshape(1).astype(jnp.int32)

    x_ring, z_ring = (x_at, X_BY, X_WITH), (z_at, Z_BY, Z_WITH)

    def along_y(low, high, *order):
        low, high = after((low, high), *order)
        return send(low, Y_UP), send(high, Y_DOWN)

    def chunk_of(v, k):
        step = v.shape[0] // 4
        return lax.dynamic_slice_in_dim(v, k * step, step, 0)

    def ring_start(v, ring, *order):
        at, by, _ = ring
        chunks = after([chunk_of(v, (at + d) % 4) for d in range(4)], *order)
        return chunks[0], [send(chunks[d], by[d]) for d in (1, 3, 2)]

    def ring_end(started):
        total = started[0].astype(F32)
        for got in started[1]:
            total = total + got.astype(F32)
        return total.astype(BF)

    def back_start(v, ring, *order):
        v = after(v, *order)
        return [v] + [send(v, ring[1][d]) for d in (1, 2, 3)]

    def back_end(pieces, ring):
        return cat([lax.select_n((ring[0] - p) % 4, *pieces) for p in range(4)])

    def halves(v):
        at = (v.shape[1] // 256) * 128
        return [(v[:, :at], 3, 1), (v[:, at:], 1, 3)]

    def fold_start(v, ring, *order):
        at, _, partner = ring
        cut = []
        for part, f, g in halves(v):
            kept = cat([chunk_of(part, at), chunk_of(part, at ^ g)])
            given = cat([chunk_of(part, at ^ f), chunk_of(part, at ^ f ^ g)])
            cut.append((kept, given))
        cut = after(cut, *order)
        return [(kept, send(given, partner[f])) for (kept, given), f in zip(cut, (3, 1))]

    def fold_next(started, ring, *order):
        sums = [(a.astype(F32) + b.astype(F32)).astype(BF) for a, b in started]
        step = sums[0].shape[0] // 2
        cut = after([(v[:step], v[step:]) for v in sums], *order)
        return [(kept, send(given, ring[2][g])) for (kept, given), g in zip(cut, (1, 3))]

    def fold_end(started):
        return cat([(a.astype(F32) + b.astype(F32)).astype(BF) for a, b in started], 1)

    def open_start(v, ring, *order):
        v = after(v, *order)
        return [(part, send(part, ring[2][g])) for part, f, g in halves(v)]

    def open_next(started, ring, *order):
        pairs = after([cat(pair) for pair in started], *order)
        return [(pair, send(pair, ring[2][f])) for pair, f in zip(pairs, (3, 1))]

    def open_end(started, ring):
        columns = []
        for (pair, got), f, g in zip(started, (3, 1), (1, 3)):
            step = pair.shape[0] // 2
            pieces = {0: pair[:step], g: pair[step:], f: got[:step], f ^ g: got[step:]}
            pieces = [pieces[k] for k in range(4)]
            columns.append(cat([lax.select_n(ring[0] ^ p, *pieces) for p in range(4)]))
        return cat(after(columns), 1)

    def joined(kept, got):
        return (kept.astype(F32) + cat(got).astype(F32)).astype(BF)

    def far_start(v, *order):
        v = after(v, *order)
        return v, send(v, Y_FAR)

    def far_end(started):
        return (started[0].astype(F32) + started[1].astype(F32)).astype(BF)

    def corner_start(v, size, summed, *order):
        first, second = v[:, :size], v[:, size : 2 * size]
        rest = v[:, 2 * size :]
        away = jnp.where(core == 0, second, first)
        mine = jnp.where(core == 0, first, second)
        if summed:
            away = cat([away, rest[:, -summed:]], 1)
        mine, away = after((cat([mine, rest], 1), away), *order)
        return mine, [send(mine, Y_FAR), send(away, CORE), send(away, FAR_CORE)]

    def corner_end(started, size, summed):
        plus = lambda a, b: a.astype(F32) + b.astype(F32)
        mine, (far, near, cross) = started
        mine, got = plus(mine, far), plus(near, cross)
        rest = mine[:, size:]
        if summed:
            rest = cat([rest[:, :-summed], rest[:, -summed:] + got[:, size:]], 1)
        low_cols = jnp.where(core == 0, mine[:, :size], got[:, :size])
        high_cols = jnp.where(core == 0, got[:, :size], mine[:, :size])
        step = 1024 if size == 2048 else 256
        cols = []
        for k in range(0, size, step):
            cols += [low_cols[:, k : k + step], high_cols[:, k : k + step]]
        return cat(cols + [rest], 1).astype(BF)

    over = lambda v: jnp.sum(v, axis=0, keepdims=True)
    down_low, down_high, down_kept = grad_of(half, act, d_low_out, 256, False)
    a_y = along_y(down_low, down_high)
    proj_down = ordered(y_lo, w_fc2, cat(d_got))
    d_hidden, sum_up = hidden_back(after(d_low_out, down_kept), proj_down, slope, 256)
    up_low, up_high, up_kept = grad_of(half, second, d_hidden, 256, True)
    d_second, d_second_low = times_rows(after(d_hidden, up_kept), proj_up, 256, [F32, BF])
    d_second = d_second + send(d_second_low, CORE).astype(F32)
    d_middle = d_out + norm_back(d_second, unit_2, scale_2, gain_2)
    d_branch = d_middle.astype(BF)
    out_low, out_high, out_kept = grad_of(half, attended, d_branch, 128, False)
    b_y = along_y(cat([up_low, out_low], 1), cat([up_high, out_high], 1))
    d_attended = dot(after(d_branch, out_kept), proj_out, ((1,), (1,))).astype(BF)
    a_v = joined(down_kept, a_y)
    a_1 = fold_start(a_v, z_ring, out_kept)
    d_attended = after(d_attended, [kept for kept, _ in a_1])
    kept_of = lambda started: [kept for kept, _ in started]
    d_qkv = after(cat(attend_back(qkv, d_attended, weights), 1), a_1)
    a_2 = fold_next(a_1, z_ring)
    d_first = dot(d_qkv, proj_qkv, ((1,), (1,)))
    sum_gain_1, sum_shift_1 = over(d_first * unit_1), over(d_first)
    qkv_low, qkv_high, qkv_kept = grad_of(
        half, first, after(d_qkv, kept_of(a_2), sum_gain_1, sum_shift_1), 256, True
    )

    once = (core == 0).astype(F32)
    hot = [(core == 0).astype(F32), (core == 1).astype(F32)]

    def spread(v, step, at):
        runs = [v[:, step * y + at : step * y + at + 256] for y in range(2)]
        return cat([runs[y] * hot[c] for y in range(2) for c in range(2)], 1)

    ones = jnp.ones((16, rows), BF)
    over_low = lambda v: dot(ones, v)[:1]
    d_qkv_sum = over_low(d_qkv)
    sums = cat(
        [
            sum_gain_1,
            sum_shift_1,
            spread(d_qkv_sum[:, :512], 256, 0),
            spread(d_qkv_sum[:, 1024:], 256, 0),
            once * over_low(d_branch),
            once * over(d_second * unit_2),
            once * over(d_second),
            once * over_low(d_low_out),
        ]
        + [spread(sum_up, 1024, 256 * k) for k in range(4)]
        + [jnp.zeros((4, 1024), F32)]
    ).astype(BF)
    packed = [
        cat([sums[:, 512 * y + 128 * k : 512 * y + 128 * k + 128] for k in range(4)])
        for y in range(2)
    ]
    given_sums = jnp.pad(jnp.where(y_lo == 0, packed[1], packed[0]), ((0, 64), (0, 0)))
    kept_sums = jnp.pad(jnp.where(y_lo == 0, packed[0], packed[1]), ((0, 192), (0, 0)))
    c_given = after(
        (cat([qkv_low, given_sums], 1), cat([qkv_high, jnp.zeros_like(given_sums)], 1)), b_y
    )
    c_y = along_y(*c_given)
    done = c_given

    b_v = joined(cat([up_kept, out_kept], 1), b_y)
    b_1 = fold_start(b_v, x_ring, done)

    d_first = after(d_first, kept_of(b_1))
    d_first_got = send(pick(d_first, 1 - core).astype(BF), CORE)
    y_part = times(after(act, d_first_got), proj_down, 256, [F32])[0]
    y_got = send(pick(y_part, 1 - core).astype(BF), CORE)
    d_first = pick(d_first, core) + d_first_got.astype(F32)
    grad_tokens = pick(d_middle, core) + norm_back(
        d_first, pick(unit_1, core), pick(scale_1, core), gain_1
    )
    out = (pick(middle, core) + pick(y_part, core) + y_got.astype(F32) + bias_down).astype(BF)

    b_2 = fold_next(b_1, x_ring, y_got, grad_tokens)
    c_v = joined(cat([qkv_kept, kept_sums], 1), c_y)
    c_1 = fold_start(c_v, z_ring, kept_of(b_2))
    c_2 = fold_next(c_1, z_ring)
    a_3 = ring_start(fold_end(a_2), x_ring, kept_of(c_2))
    b_3 = ring_start(fold_end(b_2), z_ring, kept_of(c_2))
    a_4 = far_start(ring_end(a_3), b_3[0])
    c_3 = ring_start(fold_end(c_2), x_ring, b_3[0])
    total_down = lax.all_gather(
        far_end(a_4), "replica", axis=0, tiled=True, axis_index_groups=PLANE
    ).astype(F32)
    b_4 = corner_start(ring_end(b_3), 2048, 0, c_3[0], a_4)
    c_4 = corner_start(ring_end(c_3), 1536, 128, b_4[0])
    b_5 = back_start(corner_end(b_4, 2048, 0), z_ring, c_4[0])
    c_5 = back_start(corner_end(c_4, 1536, 128), x_ring, b_5[0])
    b_6 = open_start(back_end(b_5, z_ring), x_ring, c_5[0])
    c_6 = open_start(back_end(c_5, x_ring), z_ring, kept_of(b_6))
    last = jnp.stack([out[rows_dev:].astype(F32), grad_tokens[rows_dev:]])
    last = send(after(last, kept_of(c_6)), TAIL_BACK)
    b_7 = open_next(b_6, x_ring, kept_of(c_6))
    c_7 = open_next(c_6, z_ring, kept_of(b_7))
    total = open_end(c_7, z_ring)
    total_qkv = total[:, :3072].astype(F32)
    ends = total[:64, 3072:].astype(F32)
    ends = [cat([ends[32 * c : 32 * c + 16], ends[32 * c + 16 : 32 * c + 32]], 1) for c in range(2)]
    sums = jnp.where(core == 0, ends[0], ends[1])
    total = open_end(b_7, x_ring)
    total_up, total_out = total[:, :4096].astype(F32), total[:, 4096:].astype(F32)

    local = jnp.arange(rows_dev)[:, None] + rows_dev
    swapped = (shard == 1) & (local >= IMG_LEN)

    def with_tail(v, end):
        wide = cat([v[: rows_dev - TAIL], end.astype(v.dtype)])
        return jnp.where(swapped, wide, v[:rows_dev])[None]

    return (
        with_tail(out, last[0]),
        with_tail(grad_tokens, last[1]),
        sums[0:1].reshape(256),
        sums[1:2].reshape(256),
        total_qkv,
        sums[2:3].reshape(256),
        sums[3:4].reshape(256),
        total_out,
        sums[4:5].reshape(256),
        sums[5:6].reshape(256),
        sums[6:7].reshape(256),
        total_up,
        sums[8:12].reshape(1024),
        total_down,
        sums[7:8].reshape(256),
    )


def solution(mesh):
    tokens, row, both = P("replica", "shard", None), P("shard"), P("shard", None)
    in_specs = (
        tokens, P("replica"), tokens, row, row, both, row, row, both, row, row, row, both, row,
        both, row,
    )
    out_specs = (
        tokens, tokens, row, row, both, row, row, both, row, row, row, both, row, both, row,
    )
    return jax.shard_map(body, mesh=mesh, in_specs=in_specs, out_specs=out_specs, check_vma=False)
```

```python
import jax
import jax.numpy as jnp
from jax import lax
from jax.experimental import pallas as pl
from jax.experimental.pallas import tpu as pltpu
from jax.sharding import PartitionSpec as P

HEAD_DIM = 64
IMG_LEN = 577
AXES = ("shard", "replica")
BF = jnp.bfloat16
F32 = jnp.float32
TAIL = 16


def place(index):
    shard, replica = divmod(index, 32)
    return (replica // 16) * 2 + shard // 2, (replica // 4) % 4, replica % 4, shard % 2


def index_of(y, z, x, core):
    y, z, x = y % 4, z % 4, x % 4
    return ((y % 2) * 2 + core) * 32 + (y // 2) * 16 + z * 4 + x


def moved(dy=0, dz=0, dx=0, dc=0):
    pairs = []
    for index in range(128):
        y, z, x, core = place(index)
        pairs.append((index, index_of(y + dy, z + dz, x + dx, (core + dc) % 2)))
    return pairs


CORE = moved(dc=1)
Y_UP = moved(dy=1)
Y_DOWN = moved(dy=-1)
Y_FAR = moved(dy=2)
FAR_CORE = moved(dy=2, dc=1)
X_BY = {d: moved(dx=d) for d in (1, 2, 3)}
Z_BY = {d: moved(dz=d) for d in (1, 2, 3)}
X_WITH = {d: [(i, index_of(y, z, x ^ d, c)) for i, (y, z, x, c) in enumerate(map(place, range(128)))] for d in (1, 3)}
Z_WITH = {d: [(i, index_of(y, z ^ d, x, c)) for i, (y, z, x, c) in enumerate(map(place, range(128)))] for d in (1, 3)}
PLANE = [[16 * h + k for k in range(16)] for h in range(2)]
TO_FIRST = [(32 + r, 64 + r) for r in range(32)]
TO_SECOND = [(32 + r, 96 + r) for r in range(32)]
TAIL_BACK = [(96 + r, 32 + r) for r in range(32)]


def after(value, *earlier):
    return lax.optimization_barrier((value, earlier))[0]


def send(value, pairs):
    return lax.ppermute(value, AXES, pairs)


def dot(left, right, dims=((1,), (0,))):
    return lax.dot_general(left, right, (dims, ((), ())), preferred_element_type=F32)


def normed(value):
    mean = jnp.mean(value, axis=-1, keepdims=True)
    centred = value - mean
    variance = jnp.mean(centred * centred, axis=-1, keepdims=True)
    scale = lax.rsqrt(variance + 1e-06)
    return centred * scale, scale


def norm_back(d_value, unit, scale, gain):
    t = d_value * gain
    mean_t = jnp.mean(t, axis=-1, keepdims=True)
    mean_tn = jnp.mean(t * unit, axis=-1, keepdims=True)
    return scale * (t - mean_t - unit * mean_tn)


def attend_kernel(id_col, id_row, q_ref, k_ref, v_ref, out_ref, w_ref):
    q, k, v = q_ref[...], k_ref[...], v_ref[...]
    first_head = lax.broadcasted_iota(jnp.int32, q.shape, 1) < HEAD_DIM
    same = id_col[...] == id_row[...]
    zero = jnp.zeros_like(q)
    results = []
    for head in range(2):
        mine = first_head if head == 0 else jnp.logical_not(first_head)
        scores = 0.125 * dot(jnp.where(mine, q, zero), k, ((1,), (1,)))
        scores = jnp.where(same, scores, -1e30)
        peak = jnp.max(scores, axis=-1, keepdims=True)
        expo = jnp.exp(scores - peak)
        total = jnp.sum(expo, axis=-1, keepdims=True)
        weights = (expo * (1.0 / total)).astype(BF)
        w_ref[head] = weights
        results.append(dot(weights, v))
    out_ref[...] = jnp.where(first_head, results[0], results[1]).astype(BF)


def attend(ids, qkv):
    rows = qkv.shape[0]
    pairs = qkv.shape[1] // 3 // 128
    block = lambda off: pl.BlockSpec((rows, 128), lambda h: (0, h + off))
    return pl.pallas_call(
        attend_kernel,
        grid=(pairs,),
        in_specs=[
            pl.BlockSpec((rows, 1), lambda h: (0, 0)),
            pl.BlockSpec((1, rows), lambda h: (0, 0)),
            block(0),
            block(pairs),
            block(2 * pairs),
        ],
        out_specs=[block(0), pl.BlockSpec((2, rows, rows), lambda h: (h, 0, 0))],
        out_shape=[
            jax.ShapeDtypeStruct((rows, pairs * 128), BF),
            jax.ShapeDtypeStruct((2 * pairs, rows, rows), BF),
        ],
        compiler_params=pltpu.CompilerParams(vmem_limit_bytes=48 * 2**20),
        cost_estimate=hinted(rows * rows),
    )(ids[:, None], ids[None, :], qkv, qkv, qkv)


def attend_back_kernel(q_ref, k_ref, v_ref, d_ref, w_ref, dq_ref, dk_ref, dv_ref):
    q, k, v, d_out = q_ref[...], k_ref[...], v_ref[...], d_ref[...]
    first_head = lax.broadcasted_iota(jnp.int32, q.shape, 1) < HEAD_DIM
    zero = jnp.zeros_like(q)
    parts = []
    for head in range(2):
        mine = first_head if head == 0 else jnp.logical_not(first_head)
        low = w_ref[head]
        weights = low.astype(F32)
        d_weights = dot(jnp.where(mine, d_out, zero), v, ((1,), (1,)))
        both = weights * d_weights
        d_scores = (both - weights * jnp.sum(both, axis=-1, keepdims=True)).astype(BF)
        parts.append(
            (
                dot(d_scores, k),
                dot(d_scores, q, ((0,), (0,))),
                dot(low, d_out, ((0,), (0,))),
            )
        )
    dq_ref[...] = (0.125 * jnp.where(first_head, parts[0][0], parts[1][0])).astype(BF)
    dk_ref[...] = (0.125 * jnp.where(first_head, parts[0][1], parts[1][1])).astype(BF)
    dv_ref[...] = jnp.where(first_head, parts[0][2], parts[1][2]).astype(BF)


def attend_back(qkv, d_att, weights):
    rows = qkv.shape[0]
    pairs = qkv.shape[1] // 3 // 128
    block = lambda off: pl.BlockSpec((rows, 128), lambda h: (0, h + off))
    return pl.pallas_call(
        attend_back_kernel,
        grid=(pairs,),
        in_specs=[
            block(0),
            block(pairs),
            block(2 * pairs),
            block(0),
            pl.BlockSpec((2, rows, rows), lambda h: (h, 0, 0)),
        ],
        out_specs=[block(0)] * 3,
        out_shape=[jax.ShapeDtypeStruct((rows, pairs * 128), BF)] * 3,
        compiler_params=pltpu.CompilerParams(vmem_limit_bytes=48 * 2**20),
        cost_estimate=hinted(rows * rows),
    )(qkv, qkv, qkv, d_att, weights)


def product_kernel(dims, a_ref, b_ref, *outs):
    total = dot(a_ref[...], b_ref[...], dims)
    for out in outs:
        out[...] = total.astype(out.dtype)


def hinted(flops):
    return pl.CostEstimate(flops=flops, bytes_accessed=0, transcendentals=0)


PARAMS = pltpu.CompilerParams(vmem_limit_bytes=48 * 2**20)


def times(a, b, tile, dtypes):
    rows, depth = a.shape
    cols = b.shape[1]
    return pl.pallas_call(
        lambda *refs: product_kernel(((1,), (0,)), *refs),
        grid=(cols // tile,),
        in_specs=[
            pl.BlockSpec((rows, depth), lambda i: (0, 0)),
            pl.BlockSpec((depth, tile), lambda i: (0, i)),
        ],
        out_specs=[pl.BlockSpec((rows, tile), lambda i: (0, i))] * len(dtypes),
        out_shape=[jax.ShapeDtypeStruct((rows, cols), t) for t in dtypes],
        compiler_params=PARAMS,
        cost_estimate=hinted(rows * depth),
    )(a, b)


def times_rows(a, b, tile, dtypes):
    rows, depth = a.shape
    cols = b.shape[0]
    return pl.pallas_call(
        lambda *refs: product_kernel(((1,), (1,)), *refs),
        grid=(cols // tile,),
        in_specs=[
            pl.BlockSpec((rows, depth), lambda i: (0, 0)),
            pl.BlockSpec((tile, depth), lambda i: (i, 0)),
        ],
        out_specs=[pl.BlockSpec((rows, tile), lambda i: (0, i))] * len(dtypes),
        out_shape=[jax.ShapeDtypeStruct((rows, cols), t) for t in dtypes],
        compiler_params=PARAMS,
        cost_estimate=hinted(rows * depth),
    )(a, b)


def grad_of(half, a, b, tile, side):
    rows, depth = a.shape
    cols = b.shape[1]
    tiles = depth // tile
    quarter = tiles // 4

    def kernel(half_ref, a_ref, b_ref, low, high, kept):
        i = pl.program_id(0)
        total = dot(a_ref[...], b_ref[...], ((0,), (0,))).astype(BF)

        if side:

            @pl.when(i < 2)
            def _():
                low[...] = total[: tile // 2]
                high[...] = total[tile // 2 :]

        else:

            @pl.when(i < quarter)
            def _():
                low[...] = total

            @pl.when((i >= quarter) & (i < 2 * quarter))
            def _():
                high[...] = total

        @pl.when(i >= tiles // 2)
        def _():
            kept[...] = total

    if side:
        specs = [
            pl.BlockSpec((tile // 2, cols), lambda i, h: (0, jnp.minimum(i, 1))),
            pl.BlockSpec((tile // 2, cols), lambda i, h: (0, jnp.minimum(i, 1))),
            pl.BlockSpec((tile, cols), lambda i, h: (0, jnp.maximum(i - 2, 0))),
        ]
        shapes = [(tile // 2, 2 * cols), (tile // 2, 2 * cols), (tile, 2 * cols)]
    else:
        specs = [
            pl.BlockSpec((tile, cols), lambda i, h: (jnp.minimum(i, quarter - 1), 0)),
            pl.BlockSpec((tile, cols), lambda i, h: (jnp.clip(i - quarter, 0, quarter - 1), 0)),
            pl.BlockSpec((tile, cols), lambda i, h: (jnp.maximum(i - 2 * quarter, 0), 0)),
        ]
        shapes = [(depth // 4, cols), (depth // 4, cols), (depth // 2, cols)]
    return pl.pallas_call(
        kernel,
        grid_spec=pltpu.PrefetchScalarGridSpec(
            num_scalar_prefetch=1,
            grid=(tiles,),
            in_specs=[
                pl.BlockSpec((rows, tile), lambda i, h: (0, (i + h[0] * (tiles // 2)) % tiles)),
                pl.BlockSpec((rows, cols), lambda i, h: (0, 0)),
            ],
            out_specs=specs,
        ),
        out_shape=[jax.ShapeDtypeStruct(t, BF) for t in shapes],
        compiler_params=PARAMS,
        cost_estimate=hinted(rows * depth),
    )(half, a, b)


def hidden_back(a, b, slope, tile):
    rows, depth = a.shape
    cols = b.shape[0]

    def kernel(a_ref, b_ref, slope_ref, out, sums):
        total = dot(a_ref[...], b_ref[...], ((1,), (1,))) * slope_ref[...].astype(F32)
        low = total.astype(BF)
        out[...] = low
        sums[...] = jnp.sum(low.astype(F32), axis=0, keepdims=True)

    return pl.pallas_call(
        kernel,
        grid=(cols // tile,),
        in_specs=[
            pl.BlockSpec((rows, depth), lambda i: (0, 0)),
            pl.BlockSpec((tile, depth), lambda i: (i, 0)),
            pl.BlockSpec((rows, tile), lambda i: (0, i)),
        ],
        out_specs=[
            pl.BlockSpec((rows, tile), lambda i: (0, i)),
            pl.BlockSpec((1, tile), lambda i: (0, i)),
        ],
        out_shape=[
            jax.ShapeDtypeStruct((rows, cols), BF),
            jax.ShapeDtypeStruct((1, cols), F32),
        ],
        compiler_params=PARAMS,
        cost_estimate=hinted(rows * depth),
    )(a, b, slope)


def body(
    tokens,
    image_count,
    cotangent,
    ln1_gain,
    ln1_bias,
    w_qkv,
    b_query,
    b_value,
    w_out,
    b_out,
    ln2_gain,
    ln2_bias,
    w_fc1,
    b_fc1,
    w_fc2,
    b_fc2,
):
    shard = lax.axis_index("shard")
    replica = lax.axis_index("replica")
    y_lo, core = shard // 2, shard % 2
    x_at, z_at = replica % 4, (replica // 4) % 4
    width = tokens.shape[2]
    rows_dev = tokens.shape[1]
    rows = 2 * rows_dev + TAIL
    mine = rows_dev + TAIL

    def ordered(flag, own, other, axis=0):
        return jnp.where(
            flag == 0,
            jnp.concatenate([own, other], axis),
            jnp.concatenate([other, own], axis),
        )

    cat = lambda parts, axis=0: jnp.concatenate(parts, axis)

    def blocks_of(w, size, parity):
        return cat([w[:, k : k + size] for k in range(parity * size, w.shape[1], 2 * size)], 1)

    def by_core(w, size, part):
        return jnp.where(part == 0, blocks_of(w, size, 0), blocks_of(w, size, 1))

    def across(w):
        half = w.shape[0] // 2
        return send(w[:half], Y_UP), send(w[half:], Y_DOWN)

    def columns(w, got, size):
        there = cat(got)
        pair = send(cat([by_core(w, size, 1 - core), by_core(there, size, 1 - core)]), CORE)
        rows_one = w.shape[0]
        here = ordered(core, by_core(w, size, core), pair[:rows_one])
        there = ordered(core, by_core(there, size, core), pair[rows_one:])
        return ordered(y_lo, here, there)

    own = (tokens[0], cotangent[0])
    q_got = across(w_qkv)
    other_tokens = send(own[0], CORE)
    own_tail = jnp.stack([v[rows_dev - TAIL :] for v in own])
    tail_low, tail_high = send(own_tail, TO_FIRST), send(own_tail, TO_SECOND)
    u_got = across(after(w_fc1, q_got))
    w_qkv, tail_low, own_tokens = after((w_qkv, tail_low, own[0]), q_got)
    own = (own_tokens, own[1])

    small = jnp.stack(
        [ln1_gain, ln1_bias, b_query, b_value, b_out, ln2_gain, ln2_bias, b_fc2]
        + [b_fc1[256 * k : 256 * k + 256] for k in range(4)]
    )
    small = lax.all_gather(small, "shard", axis=0).astype(F32)
    vector = lambda k: small[:, k].reshape(-1)
    core_part = lambda v: by_core(v[None], v.shape[0] // 4, core)[0]
    gain_1, shift_1, bias_out = vector(0), vector(1), vector(4)
    gain_2, shift_2, bias_down = vector(5), vector(6), vector(7)
    bias_query, bias_value = core_part(vector(2)), core_part(vector(3))
    bias_up = core_part(small[:, 8:12].reshape(-1))

    tail = jnp.where(core == 0, tail_low, tail_high)
    proj_qkv = columns(w_qkv, q_got, 256)
    whole = lambda k, other: cat([ordered(core, own[k], other), tail[k]])
    at = jnp.arange(rows)
    chip_rows = 2 * rows_dev
    second_end = 2 * IMG_LEN - chip_rows
    ids_first = jnp.where(at < IMG_LEN, 0, 1)
    ids_second = jnp.where(
        (at < second_end) | (at > chip_rows), 0, jnp.where(at == chip_rows, 2, 1)
    )
    ids = jnp.where(y_lo == 0, ids_first, ids_second)
    valid = ((ids == 0) & (image_count[0] > y_lo)).astype(F32)

    value = whole(0, other_tokens).astype(F32)
    unit_1, scale_1 = normed(value)
    first = (unit_1 * gain_1 + shift_1).astype(BF)
    packed = dot(first, proj_qkv)
    qkv = (packed + jnp.concatenate([bias_query, jnp.zeros_like(bias_query), bias_value])).astype(
        BF
    )
    o_got = across(after(w_out, qkv))
    cot_other = send(after(own[1], qkv), CORE)
    attended, weights = attend(ids, qkv)
    proj_out = ordered(y_lo, w_out, cat(o_got))
    u_got = after(u_got, attended)
    d_got = across(after(w_fc2, u_got))
    proj_up = columns(w_fc1, u_got, 1024)
    z_part = dot(attended, proj_out)
    middle = value + z_part + send(z_part.astype(BF), CORE).astype(F32) + bias_out
    unit_2, scale_2 = normed(middle)
    second = (unit_2 * gain_2 + shift_2).astype(BF)
    hidden = dot(second, proj_up) + bias_up
    cdf = 0.5 * (1.0 + lax.erf(hidden * (0.5**0.5)))
    act = (hidden * cdf).astype(BF)
    slope = (cdf + hidden * (0.3989422804014327 * jnp.exp(-0.5 * hidden * hidden))).astype(BF)

    pick = lambda v, who: lax.dynamic_slice_in_dim(v, who * rows_dev, mine, 0)
    d_out = whole(1, cot_other).astype(F32) * valid[:, None]
    d_low_out = d_out.astype(BF)
    half = (1 - y_lo).reshape(1).astype(jnp.int32)

    x_ring, z_ring = (x_at, X_BY, X_WITH), (z_at, Z_BY, Z_WITH)

    def along_y(low, high, *order):
        low, high = after((low, high), *order)
        return send(low, Y_UP), send(high, Y_DOWN)

    def chunk_of(v, k):
        step = v.shape[0] // 4
        return lax.dynamic_slice_in_dim(v, k * step, step, 0)

    def ring_start(v, ring, *order):
        at, by, _ = ring
        chunks = after([chunk_of(v, (at + d) % 4) for d in range(4)], *order)
        return chunks[0], [send(chunks[d], by[d]) for d in (1, 3, 2)]

    def ring_end(started):
        total = started[0].astype(F32)
        for got in started[1]:
            total = total + got.astype(F32)
        return total.astype(BF)

    def back_start(v, ring, *order):
        v = after(v, *order)
        return [v] + [send(v, ring[1][d]) for d in (1, 2, 3)]

    def back_end(pieces, ring):
        return cat([lax.select_n((ring[0] - p) % 4, *pieces) for p in range(4)])

    def halves(v):
        at = (v.shape[1] // 256) * 128
        return [(v[:, :at], 3, 1), (v[:, at:], 1, 3)]

    def fold_start(v, ring, *order):
        at, _, partner = ring
        cut = []
        for part, f, g in halves(v):
            kept = cat([chunk_of(part, at), chunk_of(part, at ^ g)])
            given = cat([chunk_of(part, at ^ f), chunk_of(part, at ^ f ^ g)])
            cut.append((kept, given))
        cut = after(cut, *order)
        return [(kept, send(given, partner[f])) for (kept, given), f in zip(cut, (3, 1))]

    def fold_next(started, ring, *order):
        sums = [(a.astype(F32) + b.astype(F32)).astype(BF) for a, b in started]
        step = sums[0].shape[0] // 2
        cut = after([(v[:step], v[step:]) for v in sums], *order)
        return [(kept, send(given, ring[2][g])) for (kept, given), g in zip(cut, (1, 3))]

    def fold_end(started):
        return cat([(a.astype(F32) + b.astype(F32)).astype(BF) for a, b in started], 1)

    def open_start(v, ring, *order):
        v = after(v, *order)
        return [(part, send(part, ring[2][g])) for part, f, g in halves(v)]

    def open_next(started, ring, *order):
        pairs = after([cat(pair) for pair in started], *order)
        return [(pair, send(pair, ring[2][f])) for pair, f in zip(pairs, (3, 1))]

    def open_end(started, ring):
        columns = []
        for (pair, got), f, g in zip(started, (3, 1), (1, 3)):
            step = pair.shape[0] // 2
            pieces = {0: pair[:step], g: pair[step:], f: got[:step], f ^ g: got[step:]}
            pieces = [pieces[k] for k in range(4)]
            columns.append(cat([lax.select_n(ring[0] ^ p, *pieces) for p in range(4)]))
        return cat(after(columns), 1)

    def joined(kept, got):
        return (kept.astype(F32) + cat(got).astype(F32)).astype(BF)

    def far_start(v, *order):
        v = after(v, *order)
        return v, send(v, Y_FAR)

    def far_end(started):
        return (started[0].astype(F32) + started[1].astype(F32)).astype(BF)

    def corner_start(v, size, summed, *order):
        first, second = v[:, :size], v[:, size : 2 * size]
        rest = v[:, 2 * size :]
        away = jnp.where(core == 0, second, first)
        mine = jnp.where(core == 0, first, second)
        if summed:
            away = cat([away, rest[:, -summed:]], 1)
        mine, away = after((cat([mine, rest], 1), away), *order)
        return mine, [send(mine, Y_FAR), send(away, CORE), send(away, FAR_CORE)]

    def corner_end(started, size, summed):
        plus = lambda a, b: a.astype(F32) + b.astype(F32)
        mine, (far, near, cross) = started
        mine, got = plus(mine, far), plus(near, cross)
        rest = mine[:, size:]
        if summed:
            rest = cat([rest[:, :-summed], rest[:, -summed:] + got[:, size:]], 1)
        low_cols = jnp.where(core == 0, mine[:, :size], got[:, :size])
        high_cols = jnp.where(core == 0, got[:, :size], mine[:, :size])
        step = 1024 if size == 2048 else 256
        cols = []
        for k in range(0, size, step):
            cols += [low_cols[:, k : k + step], high_cols[:, k : k + step]]
        return cat(cols + [rest], 1).astype(BF)

    over = lambda v: jnp.sum(v, axis=0, keepdims=True)
    down_low, down_high, down_kept = grad_of(half, act, d_low_out, 512, False)
    a_y = along_y(down_low, down_high)
    proj_down = ordered(y_lo, w_fc2, cat(d_got))
    d_hidden, sum_up = hidden_back(after(d_low_out, down_kept), proj_down, slope, 512)
    up_low, up_high, up_kept = grad_of(half, second, d_hidden, 256, True)
    d_second, d_second_low = times_rows(after(d_hidden, up_kept), proj_up, 512, [F32, BF])
    d_second = d_second + send(after(d_second_low, a_y), CORE).astype(F32)
    d_middle = d_out + norm_back(d_second, unit_2, scale_2, gain_2)
    d_branch = d_middle.astype(BF)
    out_low, out_high, out_kept = grad_of(half, attended, d_branch, 128, False)
    b_y = along_y(cat([up_low, out_low], 1), cat([up_high, out_high], 1))
    d_attended = dot(after(d_branch, out_kept), proj_out, ((1,), (1,))).astype(BF)
    a_v = joined(down_kept, a_y)
    a_1 = fold_start(a_v, z_ring, out_kept)
    d_attended = after(d_attended, [kept for kept, _ in a_1])
    kept_of = lambda started: [kept for kept, _ in started]
    d_qkv = after(cat(attend_back(qkv, d_attended, weights), 1), a_1)
    d_first = dot(d_qkv, proj_qkv, ((1,), (1,)))
    sum_gain_1, sum_shift_1 = over(d_first * unit_1), over(d_first)
    qkv_low, qkv_high, qkv_kept = grad_of(
        half, first, after(d_qkv, sum_gain_1, sum_shift_1), 256, True
    )

    once = (core == 0).astype(F32)
    hot = [(core == 0).astype(F32), (core == 1).astype(F32)]

    def spread(v, step, at):
        runs = [v[:, step * y + at : step * y + at + 256] for y in range(2)]
        return cat([runs[y] * hot[c] for y in range(2) for c in range(2)], 1)

    ones = jnp.ones((16, rows), BF)
    over_low = lambda v: dot(ones, v)[:1]
    d_qkv_sum = over_low(d_qkv)
    sums = cat(
        [
            sum_gain_1,
            sum_shift_1,
            spread(d_qkv_sum[:, :512], 256, 0),
            spread(d_qkv_sum[:, 1024:], 256, 0),
            once * over_low(d_branch),
            once * over(d_second * unit_2),
            once * over(d_second),
            once * over_low(d_low_out),
        ]
        + [spread(sum_up, 1024, 256 * k) for k in range(4)]
        + [jnp.zeros((4, 1024), F32)]
    ).astype(BF)
    packed = [
        cat([sums[:, 512 * y + 128 * k : 512 * y + 128 * k + 128] for k in range(4)])
        for y in range(2)
    ]
    given_sums = jnp.pad(jnp.where(y_lo == 0, packed[1], packed[0]), ((0, 64), (0, 0)))
    kept_sums = jnp.pad(jnp.where(y_lo == 0, packed[0], packed[1]), ((0, 192), (0, 0)))
    c_given = after(
        (cat([qkv_low, given_sums], 1), cat([qkv_high, jnp.zeros_like(given_sums)], 1)), a_1
    )
    c_y = along_y(*c_given)
    done = c_given
    a_2 = fold_next(a_1, z_ring, done)

    b_v = joined(cat([up_kept, out_kept], 1), after(b_y, kept_of(a_2)))
    b_1 = fold_start(b_v, x_ring)

    c_v = joined(cat([qkv_kept, kept_sums], 1), after(c_y, b_1))
    c_1 = fold_start(c_v, z_ring)
    b_2 = fold_next(b_1, x_ring, kept_of(c_1))

    y_part = times(after(act, kept_of(b_2)), proj_down, 512, [F32])[0]
    c_2 = fold_next(c_1, z_ring)
    b_3 = ring_start(fold_end(b_2), z_ring, kept_of(c_2), y_part)
    c_3 = ring_start(fold_end(c_2), x_ring, b_3[0])
    a_3 = ring_start(fold_end(a_2), x_ring, c_3[0])
    b_4 = corner_start(ring_end(b_3), 2048, 0, a_3[0])
    a_4 = far_start(ring_end(a_3), b_4[0])
    d_first = after(d_first, c_3[0])
    d_first_got = send(pick(d_first, 1 - core).astype(BF), CORE)
    y_got = send(after(pick(y_part, 1 - core).astype(BF), c_3[0]), CORE)
    d_first = pick(d_first, core) + d_first_got.astype(F32)
    grad_tokens = pick(d_middle, core) + norm_back(
        d_first, pick(unit_1, core), pick(scale_1, core), gain_1
    )
    out = (pick(middle, core) + pick(y_part, core) + y_got.astype(F32) + bias_down).astype(BF)

    total_down = lax.all_gather(
        far_end(a_4), "replica", axis=0, tiled=True, axis_index_groups=PLANE
    ).astype(F32)
    c_4 = corner_start(ring_end(c_3), 1536, 128, b_4[0])
    b_5 = back_start(corner_end(b_4, 2048, 0), z_ring, c_4[0])
    c_5 = back_start(corner_end(c_4, 1536, 128), x_ring, b_5[0])
    b_6 = open_start(back_end(b_5, z_ring), x_ring, c_5[0])
    c_6 = open_start(back_end(c_5, x_ring), z_ring, kept_of(b_6))
    last = jnp.stack([out[rows_dev:].astype(F32), grad_tokens[rows_dev:]])
    last = send(after(last, kept_of(c_6)), TAIL_BACK)
    b_7 = open_next(b_6, x_ring, kept_of(c_6))
    c_7 = open_next(c_6, z_ring, kept_of(b_7))
    total = open_end(c_7, z_ring)
    total_qkv = total[:, :3072].astype(F32)
    ends = total[:64, 3072:].astype(F32)
    ends = [cat([ends[32 * c : 32 * c + 16], ends[32 * c + 16 : 32 * c + 32]], 1) for c in range(2)]
    sums = jnp.where(core == 0, ends[0], ends[1])
    total = open_end(b_7, x_ring)
    total_up, total_out = total[:, :4096].astype(F32), total[:, 4096:].astype(F32)

    local = jnp.arange(rows_dev)[:, None] + rows_dev
    swapped = (shard == 1) & (local >= IMG_LEN)

    def with_tail(v, end):
        wide = cat([v[: rows_dev - TAIL], end.astype(v.dtype)])
        return jnp.where(swapped, wide, v[:rows_dev])[None]

    return (
        with_tail(out, last[0]),
        with_tail(grad_tokens, last[1]),
        sums[0:1].reshape(256),
        sums[1:2].reshape(256),
        total_qkv,
        sums[2:3].reshape(256),
        sums[3:4].reshape(256),
        total_out,
        sums[4:5].reshape(256),
        sums[5:6].reshape(256),
        sums[6:7].reshape(256),
        total_up,
        sums[8:12].reshape(1024),
        total_down,
        sums[7:8].reshape(256),
    )


def solution(mesh):
    tokens, row, both = P("replica", "shard", None), P("shard"), P("shard", None)
    in_specs = (
        tokens, P("replica"), tokens, row, row, both, row, row, both, row, row, row, both, row,
        both, row,
    )
    out_specs = (
        tokens, tokens, row, row, both, row, row, both, row, row, row, both, row, both, row,
    )
    return jax.shard_map(body, mesh=mesh, in_specs=in_specs, out_specs=out_specs, check_vma=False)
```

```python
import jax
import jax.numpy as jnp
from jax import lax
from jax.experimental import pallas as pl
from jax.experimental.pallas import tpu as pltpu
from jax.sharding import PartitionSpec as P

HEAD_DIM = 64
IMG_LEN = 577
AXES = ("shard", "replica")
BF = jnp.bfloat16
F32 = jnp.float32
TAIL = 16


def place(index):
    shard, replica = divmod(index, 32)
    return (replica // 16) * 2 + shard // 2, (replica // 4) % 4, replica % 4, shard % 2


def index_of(y, z, x, core):
    y, z, x = y % 4, z % 4, x % 4
    return ((y % 2) * 2 + core) * 32 + (y // 2) * 16 + z * 4 + x


def moved(dy=0, dz=0, dx=0, dc=0):
    pairs = []
    for index in range(128):
        y, z, x, core = place(index)
        pairs.append((index, index_of(y + dy, z + dz, x + dx, (core + dc) % 2)))
    return pairs


CORE = moved(dc=1)
Y_UP = moved(dy=1)
Y_DOWN = moved(dy=-1)
Y_FAR = moved(dy=2)
FAR_CORE = moved(dy=2, dc=1)
X_BY = {d: moved(dx=d) for d in (1, 2, 3)}
Z_BY = {d: moved(dz=d) for d in (1, 2, 3)}
X_WITH = {d: [(i, index_of(y, z, x ^ d, c)) for i, (y, z, x, c) in enumerate(map(place, range(128)))] for d in (1, 3)}
Z_WITH = {d: [(i, index_of(y, z ^ d, x, c)) for i, (y, z, x, c) in enumerate(map(place, range(128)))] for d in (1, 3)}
PLANE = [[16 * h + k for k in range(16)] for h in range(2)]
TO_FIRST = [(32 + r, 64 + r) for r in range(32)]
TO_SECOND = [(32 + r, 96 + r) for r in range(32)]
TAIL_BACK = [(96 + r, 32 + r) for r in range(32)]


def after(value, *earlier):
    return lax.optimization_barrier((value, earlier))[0]


def send(value, pairs):
    return lax.ppermute(value, AXES, pairs)


def dot(left, right, dims=((1,), (0,))):
    return lax.dot_general(left, right, (dims, ((), ())), preferred_element_type=F32)


def normed(value):
    mean = jnp.mean(value, axis=-1, keepdims=True)
    centred = value - mean
    variance = jnp.mean(centred * centred, axis=-1, keepdims=True)
    scale = lax.rsqrt(variance + 1e-06)
    return centred * scale, scale


def norm_back(d_value, unit, scale, gain):
    t = d_value * gain
    mean_t = jnp.mean(t, axis=-1, keepdims=True)
    mean_tn = jnp.mean(t * unit, axis=-1, keepdims=True)
    return scale * (t - mean_t - unit * mean_tn)


def attend_kernel(id_col, id_row, q_ref, k_ref, v_ref, out_ref, w_ref):
    q, k, v = q_ref[...], k_ref[...], v_ref[...]
    first_head = lax.broadcasted_iota(jnp.int32, q.shape, 1) < HEAD_DIM
    same = id_col[...] == id_row[...]
    zero = jnp.zeros_like(q)
    results = []
    for head in range(2):
        mine = first_head if head == 0 else jnp.logical_not(first_head)
        scores = 0.125 * dot(jnp.where(mine, q, zero), k, ((1,), (1,)))
        scores = jnp.where(same, scores, -1e30)
        peak = jnp.max(scores, axis=-1, keepdims=True)
        expo = jnp.exp(scores - peak)
        total = jnp.sum(expo, axis=-1, keepdims=True)
        weights = (expo * (1.0 / total)).astype(BF)
        w_ref[head] = weights
        results.append(dot(weights, v))
    out_ref[...] = jnp.where(first_head, results[0], results[1]).astype(BF)


def attend(ids, qkv):
    rows = qkv.shape[0]
    pairs = qkv.shape[1] // 3 // 128
    block = lambda off: pl.BlockSpec((rows, 128), lambda h: (0, h + off))
    return pl.pallas_call(
        attend_kernel,
        grid=(pairs,),
        in_specs=[
            pl.BlockSpec((rows, 1), lambda h: (0, 0)),
            pl.BlockSpec((1, rows), lambda h: (0, 0)),
            block(0),
            block(pairs),
            block(2 * pairs),
        ],
        out_specs=[block(0), pl.BlockSpec((2, rows, rows), lambda h: (h, 0, 0))],
        out_shape=[
            jax.ShapeDtypeStruct((rows, pairs * 128), BF),
            jax.ShapeDtypeStruct((2 * pairs, rows, rows), BF),
        ],
        compiler_params=pltpu.CompilerParams(vmem_limit_bytes=48 * 2**20),
        cost_estimate=hinted(rows * rows),
    )(ids[:, None], ids[None, :], qkv, qkv, qkv)


def attend_back_kernel(q_ref, k_ref, v_ref, d_ref, w_ref, dq_ref, dk_ref, dv_ref):
    q, k, v, d_out = q_ref[...], k_ref[...], v_ref[...], d_ref[...]
    first_head = lax.broadcasted_iota(jnp.int32, q.shape, 1) < HEAD_DIM
    zero = jnp.zeros_like(q)
    parts = []
    for head in range(2):
        mine = first_head if head == 0 else jnp.logical_not(first_head)
        low = w_ref[head]
        weights = low.astype(F32)
        d_weights = dot(jnp.where(mine, d_out, zero), v, ((1,), (1,)))
        both = weights * d_weights
        d_scores = (both - weights * jnp.sum(both, axis=-1, keepdims=True)).astype(BF)
        parts.append(
            (
                dot(d_scores, k),
                dot(d_scores, q, ((0,), (0,))),
                dot(low, d_out, ((0,), (0,))),
            )
        )
    dq_ref[...] = (0.125 * jnp.where(first_head, parts[0][0], parts[1][0])).astype(BF)
    dk_ref[...] = (0.125 * jnp.where(first_head, parts[0][1], parts[1][1])).astype(BF)
    dv_ref[...] = jnp.where(first_head, parts[0][2], parts[1][2]).astype(BF)


def attend_back(qkv, d_att, weights):
    rows = qkv.shape[0]
    pairs = qkv.shape[1] // 3 // 128
    block = lambda off: pl.BlockSpec((rows, 128), lambda h: (0, h + off))
    return pl.pallas_call(
        attend_back_kernel,
        grid=(pairs,),
        in_specs=[
            block(0),
            block(pairs),
            block(2 * pairs),
            block(0),
            pl.BlockSpec((2, rows, rows), lambda h: (h, 0, 0)),
        ],
        out_specs=[block(0)] * 3,
        out_shape=[jax.ShapeDtypeStruct((rows, pairs * 128), BF)] * 3,
        compiler_params=pltpu.CompilerParams(vmem_limit_bytes=48 * 2**20),
        cost_estimate=hinted(rows * rows),
    )(qkv, qkv, qkv, d_att, weights)


def product_kernel(dims, a_ref, b_ref, *outs):
    total = dot(a_ref[...], b_ref[...], dims)
    for out in outs:
        out[...] = total.astype(out.dtype)


def hinted(flops):
    return pl.CostEstimate(flops=flops, bytes_accessed=0, transcendentals=0)


PARAMS = pltpu.CompilerParams(vmem_limit_bytes=48 * 2**20)


def times(a, b, tile, dtypes):
    rows, depth = a.shape
    cols = b.shape[1]
    return pl.pallas_call(
        lambda *refs: product_kernel(((1,), (0,)), *refs),
        grid=(cols // tile,),
        in_specs=[
            pl.BlockSpec((rows, depth), lambda i: (0, 0)),
            pl.BlockSpec((depth, tile), lambda i: (0, i)),
        ],
        out_specs=[pl.BlockSpec((rows, tile), lambda i: (0, i))] * len(dtypes),
        out_shape=[jax.ShapeDtypeStruct((rows, cols), t) for t in dtypes],
        compiler_params=PARAMS,
        cost_estimate=hinted(rows * depth),
    )(a, b)


def times_rows(a, b, tile, dtypes):
    rows, depth = a.shape
    cols = b.shape[0]
    return pl.pallas_call(
        lambda *refs: product_kernel(((1,), (1,)), *refs),
        grid=(cols // tile,),
        in_specs=[
            pl.BlockSpec((rows, depth), lambda i: (0, 0)),
            pl.BlockSpec((tile, depth), lambda i: (i, 0)),
        ],
        out_specs=[pl.BlockSpec((rows, tile), lambda i: (0, i))] * len(dtypes),
        out_shape=[jax.ShapeDtypeStruct((rows, cols), t) for t in dtypes],
        compiler_params=PARAMS,
        cost_estimate=hinted(rows * depth),
    )(a, b)


def grad_of(half, a, b, tile, side):
    rows, depth = a.shape
    cols = b.shape[1]
    tiles = depth // tile
    quarter = tiles // 4

    def kernel(half_ref, a_ref, b_ref, low, high, kept):
        i = pl.program_id(0)
        total = dot(a_ref[...], b_ref[...], ((0,), (0,))).astype(BF)

        if side:

            @pl.when(i < 2)
            def _():
                low[...] = total[: tile // 2]
                high[...] = total[tile // 2 :]

        else:

            @pl.when(i < quarter)
            def _():
                low[...] = total

            @pl.when((i >= quarter) & (i < 2 * quarter))
            def _():
                high[...] = total

        @pl.when(i >= tiles // 2)
        def _():
            kept[...] = total

    if side:
        specs = [
            pl.BlockSpec((tile // 2, cols), lambda i, h: (0, jnp.minimum(i, 1))),
            pl.BlockSpec((tile // 2, cols), lambda i, h: (0, jnp.minimum(i, 1))),
            pl.BlockSpec((tile, cols), lambda i, h: (0, jnp.maximum(i - 2, 0))),
        ]
        shapes = [(tile // 2, 2 * cols), (tile // 2, 2 * cols), (tile, 2 * cols)]
    else:
        specs = [
            pl.BlockSpec((tile, cols), lambda i, h: (jnp.minimum(i, quarter - 1), 0)),
            pl.BlockSpec((tile, cols), lambda i, h: (jnp.clip(i - quarter, 0, quarter - 1), 0)),
            pl.BlockSpec((tile, cols), lambda i, h: (jnp.maximum(i - 2 * quarter, 0), 0)),
        ]
        shapes = [(depth // 4, cols), (depth // 4, cols), (depth // 2, cols)]
    return pl.pallas_call(
        kernel,
        grid_spec=pltpu.PrefetchScalarGridSpec(
            num_scalar_prefetch=1,
            grid=(tiles,),
            in_specs=[
                pl.BlockSpec((rows, tile), lambda i, h: (0, (i + h[0] * (tiles // 2)) % tiles)),
                pl.BlockSpec((rows, cols), lambda i, h: (0, 0)),
            ],
            out_specs=specs,
        ),
        out_shape=[jax.ShapeDtypeStruct(t, BF) for t in shapes],
        compiler_params=PARAMS,
        cost_estimate=hinted(rows * depth),
    )(half, a, b)


def hidden_back(a, b, slope, tile):
    rows, depth = a.shape
    cols = b.shape[0]

    def kernel(a_ref, b_ref, slope_ref, out, sums):
        total = dot(a_ref[...], b_ref[...], ((1,), (1,))) * slope_ref[...].astype(F32)
        low = total.astype(BF)
        out[...] = low
        sums[...] = jnp.sum(low.astype(F32), axis=0, keepdims=True)

    return pl.pallas_call(
        kernel,
        grid=(cols // tile,),
        in_specs=[
            pl.BlockSpec((rows, depth), lambda i: (0, 0)),
            pl.BlockSpec((tile, depth), lambda i: (i, 0)),
            pl.BlockSpec((rows, tile), lambda i: (0, i)),
        ],
        out_specs=[
            pl.BlockSpec((rows, tile), lambda i: (0, i)),
            pl.BlockSpec((1, tile), lambda i: (0, i)),
        ],
        out_shape=[
            jax.ShapeDtypeStruct((rows, cols), BF),
            jax.ShapeDtypeStruct((1, cols), F32),
        ],
        compiler_params=PARAMS,
        cost_estimate=hinted(rows * depth),
    )(a, b, slope)


def body(
    tokens,
    image_count,
    cotangent,
    ln1_gain,
    ln1_bias,
    w_qkv,
    b_query,
    b_value,
    w_out,
    b_out,
    ln2_gain,
    ln2_bias,
    w_fc1,
    b_fc1,
    w_fc2,
    b_fc2,
):
    shard = lax.axis_index("shard")
    replica = lax.axis_index("replica")
    y_lo, core = shard // 2, shard % 2
    x_at, z_at = replica % 4, (replica // 4) % 4
    width = tokens.shape[2]
    rows_dev = tokens.shape[1]
    rows = 2 * rows_dev + TAIL
    mine = rows_dev + TAIL

    def ordered(flag, own, other, axis=0):
        return jnp.where(
            flag == 0,
            jnp.concatenate([own, other], axis),
            jnp.concatenate([other, own], axis),
        )

    cat = lambda parts, axis=0: jnp.concatenate(parts, axis)

    def blocks_of(w, size, parity):
        return cat([w[:, k : k + size] for k in range(parity * size, w.shape[1], 2 * size)], 1)

    def by_core(w, size, part):
        return jnp.where(part == 0, blocks_of(w, size, 0), blocks_of(w, size, 1))

    def across(w):
        half = w.shape[0] // 2
        return send(w[:half], Y_UP), send(w[half:], Y_DOWN)

    def columns(w, got, size):
        there = cat(got)
        pair = send(cat([by_core(w, size, 1 - core), by_core(there, size, 1 - core)]), CORE)
        rows_one = w.shape[0]
        here = ordered(core, by_core(w, size, core), pair[:rows_one])
        there = ordered(core, by_core(there, size, core), pair[rows_one:])
        return ordered(y_lo, here, there)

    own = (tokens[0], cotangent[0])
    q_got = across(w_qkv)
    other_tokens = send(own[0], CORE)
    own_tail = jnp.stack([v[rows_dev - TAIL :] for v in own])
    tail_low, tail_high = send(own_tail, TO_FIRST), send(own_tail, TO_SECOND)
    u_got = across(after(w_fc1, q_got))
    w_qkv, tail_low, own_tokens = after((w_qkv, tail_low, own[0]), q_got)
    own = (own_tokens, own[1])

    small = jnp.stack(
        [ln1_gain, ln1_bias, b_query, b_value, b_out, ln2_gain, ln2_bias, b_fc2]
        + [b_fc1[256 * k : 256 * k + 256] for k in range(4)]
    )
    small = lax.all_gather(small, "shard", axis=0).astype(F32)
    vector = lambda k: small[:, k].reshape(-1)
    core_part = lambda v: by_core(v[None], v.shape[0] // 4, core)[0]
    gain_1, shift_1, bias_out = vector(0), vector(1), vector(4)
    gain_2, shift_2, bias_down = vector(5), vector(6), vector(7)
    bias_query, bias_value = core_part(vector(2)), core_part(vector(3))
    bias_up = core_part(small[:, 8:12].reshape(-1))

    tail = jnp.where(core == 0, tail_low, tail_high)
    proj_qkv = columns(w_qkv, q_got, 256)
    whole = lambda k, other: cat([ordered(core, own[k], other), tail[k]])
    at = jnp.arange(rows)
    chip_rows = 2 * rows_dev
    second_end = 2 * IMG_LEN - chip_rows
    ids_first = jnp.where(at < IMG_LEN, 0, 1)
    ids_second = jnp.where(
        (at < second_end) | (at > chip_rows), 0, jnp.where(at == chip_rows, 2, 1)
    )
    ids = jnp.where(y_lo == 0, ids_first, ids_second)
    valid = ((ids == 0) & (image_count[0] > y_lo)).astype(F32)

    value = whole(0, other_tokens).astype(F32)
    unit_1, scale_1 = normed(value)
    first = (unit_1 * gain_1 + shift_1).astype(BF)
    packed = dot(first, proj_qkv)
    qkv = (packed + jnp.concatenate([bias_query, jnp.zeros_like(bias_query), bias_value])).astype(
        BF
    )
    o_got = across(after(w_out, qkv))
    cot_other = send(after(own[1], qkv), CORE)
    attended, weights = attend(ids, qkv)
    proj_out = ordered(y_lo, w_out, cat(o_got))
    u_got = after(u_got, attended)
    d_got = across(after(w_fc2, u_got))
    proj_up = columns(w_fc1, u_got, 1024)
    z_part = dot(attended, proj_out)
    middle = value + z_part + send(z_part.astype(BF), CORE).astype(F32) + bias_out
    unit_2, scale_2 = normed(middle)
    second = (unit_2 * gain_2 + shift_2).astype(BF)
    hidden = dot(second, proj_up) + bias_up
    cdf = 0.5 * (1.0 + lax.erf(hidden * (0.5**0.5)))
    act = (hidden * cdf).astype(BF)
    slope = (cdf + hidden * (0.3989422804014327 * jnp.exp(-0.5 * hidden * hidden))).astype(BF)

    pick = lambda v, who: lax.dynamic_slice_in_dim(v, who * rows_dev, mine, 0)
    d_out = whole(1, cot_other).astype(F32) * valid[:, None]
    d_low_out = d_out.astype(BF)
    half = (1 - y_lo).reshape(1).astype(jnp.int32)

    x_ring, z_ring = (x_at, X_BY, X_WITH), (z_at, Z_BY, Z_WITH)

    def along_y(low, high, *order):
        low, high = after((low, high), *order)
        return send(low, Y_UP), send(high, Y_DOWN)

    def chunk_of(v, k):
        step = v.shape[0] // 4
        return lax.dynamic_slice_in_dim(v, k * step, step, 0)

    def ring_start(v, ring, *order):
        at, by, _ = ring
        chunks = after([chunk_of(v, (at + d) % 4) for d in range(4)], *order)
        return chunks[0], [send(chunks[d], by[d]) for d in (1, 3, 2)]

    def ring_end(started):
        total = started[0].astype(F32)
        for got in started[1]:
            total = total + got.astype(F32)
        return total.astype(BF)

    def back_start(v, ring, *order):
        v = after(v, *order)
        return [v] + [send(v, ring[1][d]) for d in (1, 2, 3)]

    def back_end(pieces, ring):
        return cat([lax.select_n((ring[0] - p) % 4, *pieces) for p in range(4)])

    def halves(v):
        at = (v.shape[1] // 256) * 128
        return [(v[:, :at], 3, 1), (v[:, at:], 1, 3)]

    def fold_start(v, ring, *order):
        at, _, partner = ring
        cut = []
        for part, f, g in halves(v):
            kept = cat([chunk_of(part, at), chunk_of(part, at ^ g)])
            given = cat([chunk_of(part, at ^ f), chunk_of(part, at ^ f ^ g)])
            cut.append((kept, given))
        cut = after(cut, *order)
        return [(kept, send(given, partner[f])) for (kept, given), f in zip(cut, (3, 1))]

    def fold_next(started, ring, *order):
        sums = [(a.astype(F32) + b.astype(F32)).astype(BF) for a, b in started]
        step = sums[0].shape[0] // 2
        cut = after([(v[:step], v[step:]) for v in sums], *order)
        return [(kept, send(given, ring[2][g])) for (kept, given), g in zip(cut, (1, 3))]

    def fold_end(started):
        return cat([(a.astype(F32) + b.astype(F32)).astype(BF) for a, b in started], 1)

    def open_start(v, ring, *order):
        v = after(v, *order)
        return [(part, send(part, ring[2][g])) for part, f, g in halves(v)]

    def open_next(started, ring, *order):
        pairs = after([cat(pair) for pair in started], *order)
        return [(pair, send(pair, ring[2][f])) for pair, f in zip(pairs, (3, 1))]

    def open_end(started, ring):
        columns = []
        for (pair, got), f, g in zip(started, (3, 1), (1, 3)):
            step = pair.shape[0] // 2
            pieces = {0: pair[:step], g: pair[step:], f: got[:step], f ^ g: got[step:]}
            pieces = [pieces[k] for k in range(4)]
            columns.append(cat([lax.select_n(ring[0] ^ p, *pieces) for p in range(4)]))
        return cat(after(columns), 1)

    def joined(kept, got):
        return (kept.astype(F32) + cat(got).astype(F32)).astype(BF)

    def far_start(v, *order):
        v = after(v, *order)
        return v, send(v, Y_FAR)

    def far_end(started):
        return (started[0].astype(F32) + started[1].astype(F32)).astype(BF)

    def corner_start(v, size, summed, *order):
        first, second = v[:, :size], v[:, size : 2 * size]
        rest = v[:, 2 * size :]
        away = jnp.where(core == 0, second, first)
        mine = jnp.where(core == 0, first, second)
        if summed:
            away = cat([away, rest[:, -summed:]], 1)
        mine, away = after((cat([mine, rest], 1), away), *order)
        return mine, [send(mine, Y_FAR), send(away, CORE), send(away, FAR_CORE)]

    def corner_end(started, size, summed):
        plus = lambda a, b: a.astype(F32) + b.astype(F32)
        mine, (far, near, cross) = started
        mine, got = plus(mine, far), plus(near, cross)
        rest = mine[:, size:]
        if summed:
            rest = cat([rest[:, :-summed], rest[:, -summed:] + got[:, size:]], 1)
        low_cols = jnp.where(core == 0, mine[:, :size], got[:, :size])
        high_cols = jnp.where(core == 0, got[:, :size], mine[:, :size])
        step = 1024 if size == 2048 else 256
        cols = []
        for k in range(0, size, step):
            cols += [low_cols[:, k : k + step], high_cols[:, k : k + step]]
        return cat(cols + [rest], 1).astype(BF)

    over = lambda v: jnp.sum(v, axis=0, keepdims=True)
    down_low, down_high, down_kept = grad_of(half, act, d_low_out, 512, False)
    a_y = along_y(down_low, down_high)
    proj_down = ordered(y_lo, w_fc2, cat(d_got))
    d_hidden, sum_up = hidden_back(after(d_low_out, down_kept), proj_down, slope, 512)
    up_low, up_high, up_kept = grad_of(half, second, d_hidden, 256, True)
    d_second, d_second_low = times_rows(after(d_hidden, up_kept), proj_up, 512, [F32, BF])
    d_second = d_second + send(after(d_second_low, a_y), CORE).astype(F32)
    d_middle = d_out + norm_back(d_second, unit_2, scale_2, gain_2)
    d_branch = d_middle.astype(BF)
    out_low, out_high, out_kept = grad_of(half, attended, d_branch, 128, False)
    b_y = along_y(cat([up_low, out_low], 1), cat([up_high, out_high], 1))
    d_attended = dot(after(d_branch, out_kept), proj_out, ((1,), (1,))).astype(BF)
    a_v = joined(down_kept, a_y)
    a_1 = fold_start(a_v, z_ring, out_kept)
    d_attended = after(d_attended, [kept for kept, _ in a_1])
    kept_of = lambda started: [kept for kept, _ in started]
    d_qkv = after(cat(attend_back(qkv, d_attended, weights), 1), a_1)
    d_first = dot(d_qkv, proj_qkv, ((1,), (1,)))
    sum_gain_1, sum_shift_1 = over(d_first * unit_1), over(d_first)
    qkv_low, qkv_high, qkv_kept = grad_of(
        half, first, after(d_qkv, sum_gain_1, sum_shift_1), 256, True
    )

    once = (core == 0).astype(F32)
    hot = [(core == 0).astype(F32), (core == 1).astype(F32)]

    def spread(v, step, at):
        runs = [v[:, step * y + at : step * y + at + 256] for y in range(2)]
        return cat([runs[y] * hot[c] for y in range(2) for c in range(2)], 1)

    ones = jnp.ones((16, rows), BF)
    over_low = lambda v: dot(ones, v)[:1]
    d_qkv_sum = over_low(d_qkv)
    sums = cat(
        [
            sum_gain_1,
            sum_shift_1,
            spread(d_qkv_sum[:, :512], 256, 0),
            spread(d_qkv_sum[:, 1024:], 256, 0),
            once * over_low(d_branch),
            once * over(d_second * unit_2),
            once * over(d_second),
            once * over_low(d_low_out),
        ]
        + [spread(sum_up, 1024, 256 * k) for k in range(4)]
        + [jnp.zeros((4, 1024), F32)]
    ).astype(BF)
    packed = [
        cat([sums[:, 512 * y + 128 * k : 512 * y + 128 * k + 128] for k in range(4)])
        for y in range(2)
    ]
    given_sums = jnp.pad(jnp.where(y_lo == 0, packed[1], packed[0]), ((0, 64), (0, 0)))
    kept_sums = jnp.pad(jnp.where(y_lo == 0, packed[0], packed[1]), ((0, 192), (0, 0)))
    c_given = after(
        (cat([qkv_low, given_sums], 1), cat([qkv_high, jnp.zeros_like(given_sums)], 1)), a_1
    )
    c_y = along_y(*c_given)
    done = c_given
    a_2 = fold_next(a_1, z_ring, done)

    b_v = joined(cat([up_kept, out_kept], 1), after(b_y, kept_of(a_2)))
    b_1 = fold_start(b_v, x_ring)

    c_v = joined(cat([qkv_kept, kept_sums], 1), after(c_y, b_1))
    c_1 = fold_start(c_v, z_ring)
    b_2 = fold_next(b_1, x_ring, kept_of(c_1))

    y_part = times(after(act, kept_of(b_2)), proj_down, 512, [F32])[0]
    c_2 = fold_next(c_1, z_ring)
    b_3 = ring_start(fold_end(b_2), z_ring, kept_of(c_2), y_part)
    c_3 = ring_start(fold_end(c_2), x_ring, b_3[0])
    a_3 = ring_start(fold_end(a_2), x_ring, c_3[0])
    b_4 = corner_start(ring_end(b_3), 2048, 0, a_3[0])
    a_4 = far_start(ring_end(a_3), b_4[0])
    d_first = after(d_first, c_3[0])
    d_first_got = send(pick(d_first, 1 - core).astype(BF), CORE)
    y_got = send(after(pick(y_part, 1 - core).astype(BF), c_3[0]), CORE)
    d_first = pick(d_first, core) + d_first_got.astype(F32)
    grad_tokens = pick(d_middle, core) + norm_back(
        d_first, pick(unit_1, core), pick(scale_1, core), gain_1
    )
    out = (pick(middle, core) + pick(y_part, core) + y_got.astype(F32) + bias_down).astype(BF)

    total_down = lax.all_gather(
        far_end(a_4), "replica", axis=0, tiled=True, axis_index_groups=PLANE
    ).astype(F32)
    c_4 = corner_start(ring_end(c_3), 1536, 128, b_4[0])
    b_5 = back_start(corner_end(b_4, 2048, 0), z_ring, c_4[0], out, grad_tokens)
    c_5 = back_start(corner_end(c_4, 1536, 128), x_ring, b_5[0])
    b_6 = open_start(back_end(b_5, z_ring), x_ring, c_5[0])
    c_6 = open_start(back_end(c_5, x_ring), z_ring, kept_of(b_6))
    last = jnp.stack([out[rows_dev:].astype(F32), grad_tokens[rows_dev:]])
    last = send(after(last, kept_of(c_6)), TAIL_BACK)
    b_7 = open_next(b_6, x_ring, kept_of(c_6))
    c_7 = open_next(c_6, z_ring, kept_of(b_7))
    total = open_end(c_7, z_ring)
    total_qkv = total[:, :3072].astype(F32)
    ends = total[:64, 3072:].astype(F32)
    ends = [cat([ends[32 * c : 32 * c + 16], ends[32 * c + 16 : 32 * c + 32]], 1) for c in range(2)]
    sums = jnp.where(core == 0, ends[0], ends[1])
    total = open_end(b_7, x_ring)
    total_up, total_out = total[:, :4096].astype(F32), total[:, 4096:].astype(F32)

    local = jnp.arange(rows_dev)[:, None] + rows_dev
    swapped = (shard == 1) & (local >= IMG_LEN)

    def with_tail(v, end):
        wide = cat([v[: rows_dev - TAIL], end.astype(v.dtype)])
        return jnp.where(swapped, wide, v[:rows_dev])[None]

    return (
        with_tail(out, last[0]),
        with_tail(grad_tokens, last[1]),
        sums[0:1].reshape(256),
        sums[1:2].reshape(256),
        total_qkv,
        sums[2:3].reshape(256),
        sums[3:4].reshape(256),
        total_out,
        sums[4:5].reshape(256),
        sums[5:6].reshape(256),
        sums[6:7].reshape(256),
        total_up,
        sums[8:12].reshape(1024),
        total_down,
        sums[7:8].reshape(256),
    )


def solution(mesh):
    tokens, row, both = P("replica", "shard", None), P("shard"), P("shard", None)
    in_specs = (
        tokens, P("replica"), tokens, row, row, both, row, row, both, row, row, row, both, row,
        both, row,
    )
    out_specs = (
        tokens, tokens, row, row, both, row, row, both, row, row, row, both, row, both, row,
    )
    return jax.shard_map(body, mesh=mesh, in_specs=in_specs, out_specs=out_specs, check_vma=False)
```
